32 devices in a mesh: seq: 8 (over y, x, core), head: 4 (over z).
Axes of the slice: x: 2, y: 2, z: 4, core: 2. Of those that a mesh axis runs over, the one named last changes fastest.
Arguments:
- activations: bfloat16 [4096, 5376], P(('seq', 'head')), may hold values from -42 to 42, as said below
- input_gain: float32 [5376], replicated, may hold values from 0.1 to 1.9
- query_weight: bfloat16 [5376, 4096], P(None, 'head'), may hold values from -2.2818633 to 2.2818633
- key_weight: bfloat16 [5376, 2048], P(None, 'head'), may hold values from -1 to 1
- value_weight: bfloat16 [5376, 2048], P(None, 'head'), may hold values from -0.078125 to 0.078125
- output_weight: bfloat16 [4096, 5376], P('head'), may hold values from -0.09375 to 0.09375
- cache_edge: bfloat16 [2, 1024, 2048], P(None, None, 'head'), may hold values from -6 to 6
- post_gain: float32 [5376], replicated, may hold values from 0.1 to 1.9
Outputs:
- layer_out: bfloat16 [4096, 5376], P(('seq', 'head'))
The draws below stay inside these ranges and needn't reach their ends.
Inputs may be any that keep to these rules, and one draw needn't show every extreme that they name: `activations`: input rows with row and feature scales.
All inputs are finite; a program needn't handle non-finite values.
Results may differ from the reference program's by a relative error of at most 0.006.
Values may be sent and summed in bfloat16 or wider, within the bound.
A program may use at most 128 MiB of HBM per device.

```python
import math
import jax
import jax.numpy as jnp
from jax import lax

D = 5376
QH = 32
KVH = 16
HD = 128
WINDOW = 1024
SCALAR = 168
TOK_DEV = 512
TOKENS = 4096
N_SEQ = 8


def key_matrix(key):
    base = jnp.clip(jax.random.normal(jax.random.fold_in(key, 7), (D, KVH * HD), jnp.float32), -4.0, 4.0)
    return base * D ** (-0.5)


def draw_activations(key, part):
    first, second, third = jax.random.split(key, 3)
    row_scale = jnp.exp(jax.random.uniform(first, (TOKENS, 1), jnp.float32, math.log(0.32), math.log(3.2)))
    column_scale = jnp.exp(jax.random.uniform(second, (1, D), jnp.float32, math.log(0.32), math.log(3.2)))
    base = jnp.clip(jax.random.normal(third, (TOKENS, D), jnp.float32), -4.0, 4.0)
    return (base * row_scale * column_scale).astype(jnp.bfloat16)


def draw_key_weight(key, part):
    return key_matrix(key).astype(jnp.bfloat16)


def draw_query_weight(key, part):
    base = jnp.clip(jax.random.normal(jax.random.fold_in(key, 11), (D, QH * HD), jnp.float32), -4.0, 4.0) * D ** (-0.5)
    return base.astype(jnp.bfloat16)


def shard_levels(stream_key, shape, pieces, least, top_value):
    def one(position, blocks):
        heights = jax.random.uniform(jax.random.fold_in(jax.random.fold_in(stream_key, 6), position), (blocks,), jnp.float32, least / len(pieces), top_value / len(pieces))
        return jnp.repeat(jnp.exp(heights), shape[position] // blocks).reshape((-1,) + (1,) * (len(shape) - position - 1))

    level = one(*pieces[0])
    for cut in pieces[1:]:
        level = level * one(*cut)
    return level


def normal_values(key, extent, width, bound, cuts=(), kind=jnp.bfloat16):
    loudness = shard_levels(key, extent, cuts, -0.22, 0.18) if cuts else 1.0
    values = jax.random.normal(key, extent, jnp.float32) * width * loudness
    return jnp.minimum(jnp.maximum(values, -bound), bound).astype(kind)


def setup_inputs(seed: int = 0) -> dict:
    splits = jax.random.split(jax.random.key(seed), 9)
    return {
        "activations": draw_activations(jax.random.fold_in(splits[8], 71), 0),
        "input_gain": jnp.clip(1.0 + 0.18 * jax.random.normal(splits[1], (D,), jnp.float32), 0.1, 1.9),
        "query_weight": draw_query_weight(jax.random.fold_in(splits[8], 71), 0),
        "key_weight": draw_key_weight(jax.random.fold_in(splits[8], 71), 0),
        "value_weight": normal_values(splits[4], (D, KVH * HD), D ** -0.5, 0.078125, ((1, 4),)),
        "output_weight": normal_values(splits[5], (QH * HD, D), (QH * HD) ** -0.5, 0.09375, ((0, 4),)),
        "cache_edge": normal_values(splits[6], (2, WINDOW, KVH * HD), 1.0, 6.0, ((2, 4),)),
        "post_gain": jnp.clip(1.0 + 0.18 * jax.random.normal(splits[7], (D,), jnp.float32), 0.1, 1.9),
    }


EPSILON = 1e-06
ROPE_BASE = 10000.0

def normalize_rows(values, gain):
    return values * lax.rsqrt(lax.optimization_barrier(jnp.mean(values * values, axis=-1, keepdims=True)) + EPSILON) * gain

def rotate(vectors, positions):
    half_size = vectors.shape[-1] // 2
    frequency = ROPE_BASE ** (-(jnp.arange(half_size, dtype=jnp.float32) * 2.0 / vectors.shape[-1]))
    angles = positions[:, None] * frequency[None, :]
    cosine = jnp.cos(angles)[:, None, :]
    sine_part = jnp.sin(angles)[:, None, :]
    first_half = vectors[..., :half_size]
    second_half = vectors[..., half_size:]
    return jnp.concatenate([first_half * cosine - second_half * sine_part, second_half * cosine + first_half * sine_part], axis=-1)

def reference(activations, input_gain, query_weight, key_weight, value_weight, output_weight, cache_edge, post_gain):
    residual = activations.astype(jnp.float32)
    normed = normalize_rows(residual, input_gain).astype(jnp.bfloat16)
    queries_raw = jnp.dot(normed, query_weight, preferred_element_type=jnp.float32)
    keys_raw = jnp.dot(normed, key_weight, preferred_element_type=jnp.float32)
    value_rows = jnp.dot(normed, value_weight, preferred_element_type=jnp.float32)
    positions = jnp.arange(TOKENS, dtype=jnp.int32).astype(jnp.float32)
    queries = (rotate(queries_raw.reshape(TOKENS, QH, HD), positions) * SCALAR ** (-0.5)).astype(jnp.bfloat16)
    keys = rotate(keys_raw.reshape(TOKENS, KVH, HD), positions).astype(jnp.bfloat16)
    values = value_rows.astype(jnp.bfloat16).reshape(TOKENS, KVH, HD)
    all_keys = jnp.concatenate([cache_edge[0].reshape(WINDOW, KVH, HD), keys], axis=0)
    all_values = jnp.concatenate([cache_edge[1].reshape(WINDOW, KVH, HD), values], axis=0)
    group_size = QH // KVH
    query_index = jnp.arange(TOK_DEV, dtype=jnp.int32)
    key_index = jnp.arange(WINDOW + TOK_DEV, dtype=jnp.int32)
    allowed = (key_index[None, :] > query_index[:, None]) & (key_index[None, :] <= query_index[:, None] + WINDOW)

    def one_block(block_index):
        first_row = (block_index * TOK_DEV).astype(jnp.int32)
        query_block = lax.dynamic_slice_in_dim(queries, first_row, TOK_DEV, 0).reshape(TOK_DEV, KVH, group_size, HD)
        key_block = lax.dynamic_slice_in_dim(all_keys, first_row, WINDOW + TOK_DEV, 0)
        value_block = lax.dynamic_slice_in_dim(all_values, first_row, WINDOW + TOK_DEV, 0)
        scores = jnp.einsum('qgrd,kgd->grqk', query_block.astype(jnp.float32), key_block.astype(jnp.float32))
        scores = jnp.where(allowed[None, None], scores, -jnp.inf)
        largest = lax.optimization_barrier(jnp.max(scores, axis=-1, keepdims=True))
        exps = jnp.exp(scores - largest)
        probabilities = (exps / lax.optimization_barrier(jnp.sum(exps, axis=-1, keepdims=True))).astype(jnp.bfloat16)
        attended = jnp.einsum('grqk,kgd->qgrd', probabilities.astype(jnp.float32), value_block.astype(jnp.float32))
        return attended.astype(jnp.bfloat16).reshape(TOK_DEV, QH * HD)
    attended = lax.map(one_block, jnp.arange(N_SEQ, dtype=jnp.int32)).reshape(TOKENS, QH * HD)
    projected = jnp.dot(attended, output_weight, preferred_element_type=jnp.float32)
    branch = normalize_rows(projected, post_gain)
    return (residual + branch).astype(jnp.bfloat16)
```

```python
import functools
import jax
import jax.numpy as jnp
from jax import lax
from jax.experimental import pallas as pl
from jax.experimental.pallas import tpu as pltpu
from jax.sharding import PartitionSpec as P

HD = 128
WINDOW = 1024
SCALAR = 168
TOK_DEV = 512
EPSILON = 1e-06
ROPE_BASE = 10000.0
REACH = WINDOW // TOK_DEV
COL_CHUNKS = 7
MESH = pl.DeviceIdType.MESH


def rope_tables(positions):
    half_size = HD // 2
    frequency = ROPE_BASE ** (-(jnp.arange(half_size, dtype=jnp.float32) * 2.0 / HD))
    angles = positions[:, None] * frequency[None, :]
    cosine = jnp.cos(angles)
    sine = jnp.sin(angles)
    return jnp.concatenate([cosine, cosine], axis=1), jnp.concatenate([-sine, sine], axis=1)


def kernel(
    n, s_count,
    act_ref, gain_ref, wq_hbm, wk_hbm, wv_hbm, wo_hbm, cache_hbm, post_ref, cos_ref, sin_ref,
    out_ref,
    wq, wk, wv, wo, rows, q_buf, kv, att, slots, acc,
    w_sem, cache_sem, ag_send, ag_recv, kv_send, kv_recv, rs_send, rs_recv,
):
    s = lax.axis_index("seq")
    z = lax.axis_index("head")
    R, D = act_ref.shape
    kv_width = wk.shape[1]
    heads_kv = kv_width // HD
    group = wq.shape[1] // kv_width
    row_chunks = ag_send.shape[2]
    CR = R // row_chunks
    CD = D // COL_CHUNKS

    weight_copies = [
        pltpu.make_async_copy(src, dst, w_sem.at[i])
        for i, (src, dst) in enumerate([(wk_hbm, wk), (wv_hbm, wv), (wq_hbm, wq), (wo_hbm, wo)])
    ]
    for c in weight_copies:
        c.start()

    def cache_copies(d):
        return [
            pltpu.make_async_copy(
                cache_hbm.at[i, pl.ds(pl.multiple_of(WINDOW + (s - d) * TOK_DEV, TOK_DEV), TOK_DEV), :],
                kv.at[pl.ds(WINDOW - d * TOK_DEV, TOK_DEV), pl.ds(i * kv_width, kv_width)],
                cache_sem.at[d - 1, i],
            )
            for i in range(2)
        ]

    for d in range(1, REACH + 1):
        @pl.when(s < d)
        def _():
            for c in cache_copies(d):
                c.start()

    barrier = pltpu.get_barrier_semaphore()

    def greet(cond, ds, dz):
        @pl.when(cond)
        def _():
            pl.semaphore_signal(barrier, inc=1, device_id=(s + ds, z + dz), device_id_type=MESH)

    partners = [(z > 0, 0, -1), (z < n - 1, 0, 1)]
    for d in range(1, REACH + 1):
        partners += [(s >= d, -d, 0), (s + d < s_count, d, 0)]
    for p in partners:
        greet(*p)

    def norm_chunk(i, carry):
        r0 = pl.multiple_of(i * 16, 16)
        x = act_ref[pl.ds(r0, 16), :].astype(jnp.float32)
        y = x * lax.rsqrt(jnp.mean(x * x, axis=-1, keepdims=True) + EPSILON) * gain_ref[...].reshape(1, D)
        rows[z, pl.ds(r0, 16), :] = y.astype(jnp.bfloat16)
        return carry

    pl.semaphore_wait(barrier, sum(jnp.where(p[0], 1, 0) for p in partners))

    right = lax.rem(z + 1, n)
    left = lax.rem(z + n - 1, n)

    def ag_copy(direction, block, c):
        where = rows.at[block, pl.ds(c * CR, CR), :]
        return pltpu.make_async_remote_copy(
            src_ref=where, dst_ref=where,
            send_sem=ag_send.at[direction, block, c], recv_sem=ag_recv.at[direction, block, c],
            device_id=(s, right if direction == 0 else left), device_id_type=MESH,
        )

    def kv_copy(d, block):
        r0 = pl.multiple_of(block * R, R)
        return pltpu.make_async_remote_copy(
            src_ref=kv.at[pl.ds(WINDOW + r0, R), :],
            dst_ref=kv.at[pl.ds(WINDOW - d * TOK_DEV + r0, R), :],
            send_sem=kv_send.at[d - 1, block], recv_sem=kv_recv.at[d - 1, block],
            device_id=(lax.rem(s + d, s_count), z), device_id_type=MESH,
        )

    def rs_copy(direction, block, slot, c):
        where = slots.at[slot, c]
        return pltpu.make_async_remote_copy(
            src_ref=where, dst_ref=where,
            send_sem=rs_send.at[direction, block, c], recv_sem=rs_recv.at[direction, block, c],
            device_id=(s, right if direction == 0 else left), device_id_type=MESH,
        )

    def project(block):
        r0 = pl.multiple_of(block * R, R)
        cosine = cos_ref[pl.ds(r0, R), :]
        sine = sin_ref[pl.ds(r0, R), :]

        def run(w, tile, rotary, scale, dst, dst_r0, dst_c0):
            def one(i, carry):
                c0 = pl.multiple_of(i * tile, tile)
                t = jnp.dot(rows[block], w[:, pl.ds(c0, tile)], preferred_element_type=jnp.float32)
                for h in range(tile // HD):
                    u = t[:, h * HD:(h + 1) * HD]
                    if rotary:
                        u = u * cosine + pltpu.roll(u, HD // 2, 1) * sine
                    if scale is not None:
                        u = u * scale
                    dst[pl.ds(dst_r0, R), pl.ds(pl.multiple_of(dst_c0 + c0 + h * HD, HD), HD)] = u.astype(jnp.bfloat16)
                return carry
            lax.fori_loop(0, w.shape[1] // tile, one, 0)

        tile = min(256, kv_width)
        own = pl.multiple_of(WINDOW + r0, R)
        run(wk, tile, True, None, kv, own, 0)
        run(wv, tile, False, None, kv, own, kv_width)
        for d in range(1, REACH + 1):
            @pl.when(s + d < s_count)
            def _():
                kv_copy(d, block).start()
        run(wq, 256, True, SCALAR ** (-0.5), q_buf, r0, 0)

    for c in range(row_chunks):
        lax.fori_loop(c * CR // 16, (c + 1) * CR // 16, norm_chunk, 0)

        @pl.when(z < n - 1)
        def _():
            ag_copy(0, z, c).start()

        @pl.when(z > 0)
        def _():
            ag_copy(1, z, c).start()

    for i in range(3):
        weight_copies[i].wait()
    def gather_step(t, carry):
        from_left = z - t
        from_right = z + t
        for c in range(row_chunks):
            @pl.when(from_left >= 0)
            def _():
                ag_copy(0, from_left, c).wait_recv()

                @pl.when(z < n - 1)
                def _():
                    ag_copy(0, from_left, c).start()

            @pl.when(from_right < n)
            def _():
                ag_copy(1, from_right, c).wait_recv()

                @pl.when(z > 0)
                def _():
                    ag_copy(1, from_right, c).start()

            if c == 0:
                @pl.when(from_right - 1 < n)
                def _():
                    project(from_right - 1)

        @pl.when(from_left >= 0)
        def _():
            project(from_left)
        return carry

    lax.fori_loop(1, n, gather_step, 0)

    @pl.when(z == 0)
    def _():
        project(n - 1)

    for d in range(1, REACH + 1):
        @pl.when(s < d)
        def _():
            for c in cache_copies(d):
                c.wait()

        @pl.when(s >= d)
        def _():
            lax.fori_loop(0, n, lambda b, carry: (kv_copy(d, b).wait_recv(), carry)[1], 0)
    weight_copies[3].wait()

    row_i = lax.broadcasted_iota(jnp.int32, (group * R, R), 0)
    row_i = lax.rem(row_i, R)
    col_i = lax.broadcasted_iota(jnp.int32, (group * R, R), 1)
    later = col_i > row_i
    spans = [(0, R), (R, WINDOW - R), (WINDOW, R)]

    def attend(block):
        r0 = pl.multiple_of(block * R, R)
        for g in range(heads_kv):
            q = jnp.concatenate(
                [q_buf[pl.ds(r0, R), (g * group + a) * HD:(g * group + a + 1) * HD] for a in range(group)], axis=0
            )
            scores = []
            for j, (o, w) in enumerate(spans):
                k = kv[pl.ds(pl.multiple_of(r0 + o, R), w), g * HD:(g + 1) * HD]
                sc = lax.dot_general(q, k, (((1,), (1,)), ((), ())), preferred_element_type=jnp.float32)
                if j == 0:
                    sc = jnp.where(later, sc, -jnp.inf)
                if j == 2:
                    sc = jnp.where(later, -jnp.inf, sc)
                scores.append(sc)
            m = functools.reduce(jnp.maximum, [jnp.max(x, axis=-1, keepdims=True) for x in scores])
            total = 0.0
            o_sum = 0.0
            for (o, w), sc in zip(spans, scores):
                e = jnp.exp(sc - m)
                total = total + jnp.sum(e, axis=-1, keepdims=True)
                v = kv[pl.ds(pl.multiple_of(r0 + o, R), w), kv_width + g * HD:kv_width + (g + 1) * HD]
                o_sum = o_sum + jnp.dot(e.astype(jnp.bfloat16), v, preferred_element_type=jnp.float32)
            o_sum = (o_sum / total).astype(jnp.bfloat16)
            for a in range(group):
                att[:, (g * group + a) * HD:(g * group + a + 1) * HD] = o_sum[a * R:(a + 1) * R]

    TILE = 256

    def partial_out(direction, block, incoming):
        attend(block)
        for c in range(COL_CHUNKS):
            @pl.when(incoming)
            def _():
                rs_copy(direction, block, block, c).wait_recv()

            def one(i, carry):
                c0 = pl.multiple_of(i * TILE, TILE)
                w0 = pl.multiple_of(c * CD + i * TILE, TILE)
                p = jnp.dot(att[...], wo[:, pl.ds(w0, TILE)], preferred_element_type=jnp.float32)
                before = slots[block, c, :, pl.ds(c0, TILE)].astype(jnp.float32)
                p = p + jnp.where(incoming, before, 0.0)
                slots[block, c, :, pl.ds(c0, TILE)] = p.astype(jnp.bfloat16)
                return carry
            lax.fori_loop(0, CD // TILE, one, 0)
            send_out(direction, block, c).start()

    def send_out(direction, block, c):
        if direction == 0:
            return rs_copy(0, block, block, c)
        last = jnp.where(block == z - 1, n, block)
        return pltpu.make_async_remote_copy(
            src_ref=slots.at[block, c], dst_ref=slots.at[last, c],
            send_sem=rs_send.at[1, block, c], recv_sem=rs_recv.at[1, block, c],
            device_id=(s, left), device_id_type=MESH,
        )

    def scatter_step(t, carry):
        to_right = n - t
        to_left = t - 1

        @pl.when(to_right > z)
        def _():
            partial_out(0, to_right, z > 0)

        @pl.when(to_left < z)
        def _():
            partial_out(1, to_left, z < n - 1)
        return carry

    lax.fori_loop(1, n, scatter_step, 0)

    attend(z)

    def own(i, carry):
        w0 = pl.multiple_of(i * TILE, TILE)
        acc[:, pl.ds(w0, TILE)] = jnp.dot(att[...], wo[:, pl.ds(w0, TILE)], preferred_element_type=jnp.float32)
        return carry
    lax.fori_loop(0, D // TILE, own, 0)

    for c in range(COL_CHUNKS):
        for direction, slot, cond in ((0, z, z > 0), (1, n, z < n - 1)):
            @pl.when(cond)
            def _():
                rs_copy(direction, z, slot, c).wait_recv()
                acc[:, c * CD:(c + 1) * CD] += slots[slot, c].astype(jnp.float32)

    def finish(i, carry):
        r0 = pl.multiple_of(i * 16, 16)
        x = acc[pl.ds(r0, 16), :]
        y = x * lax.rsqrt(jnp.mean(x * x, axis=-1, keepdims=True) + EPSILON) * post_ref[...].reshape(1, D)
        out_ref[pl.ds(r0, 16), :] = (act_ref[pl.ds(r0, 16), :].astype(jnp.float32) + y).astype(jnp.bfloat16)
        return carry
    lax.fori_loop(0, R // 16, finish, 0)

    def drain(b, carry):
        @pl.when((b <= z) & (z < n - 1))
        def _():
            for c in range(row_chunks):
                ag_copy(0, b, c).wait_send()

        @pl.when((b >= z) & (z > 0))
        def _():
            for c in range(row_chunks):
                ag_copy(1, b, c).wait_send()

        @pl.when(b > z)
        def _():
            for c in range(COL_CHUNKS):
                send_out(0, b, c).wait_send()

        @pl.when(b < z)
        def _():
            for c in range(COL_CHUNKS):
                send_out(1, b, c).wait_send()

        for d in range(1, REACH + 1):
            @pl.when(s + d < s_count)
            def _():
                kv_copy(d, b).wait_send()
        return carry
    lax.fori_loop(0, n, drain, 0)


def per_device(n, s_count, act, gain, wq, wk, wv, wo, cache, post):
    R, D = act.shape
    row_chunks = min(4, R // 16)
    s = lax.axis_index("seq")
    positions = (s * TOK_DEV + jnp.arange(TOK_DEV, dtype=jnp.int32)).astype(jnp.float32)
    cosine, sine = rope_tables(positions)
    bf, f32 = jnp.bfloat16, jnp.float32
    vmem = pl.BlockSpec(memory_space=pltpu.VMEM)
    hbm = pl.BlockSpec(memory_space=pl.ANY)
    dma = pltpu.SemaphoreType.DMA
    return pl.pallas_call(
        functools.partial(kernel, n, s_count),
        out_shape=jax.ShapeDtypeStruct((R, D), bf),
        in_specs=[vmem, vmem, hbm, hbm, hbm, hbm, hbm, vmem, vmem, vmem],
        out_specs=vmem,
        scratch_shapes=[
            pltpu.VMEM(wq.shape, bf),
            pltpu.VMEM(wk.shape, bf),
            pltpu.VMEM(wv.shape, bf),
            pltpu.VMEM(wo.shape, bf),
            pltpu.VMEM((n, R, D), bf),
            pltpu.VMEM((TOK_DEV, wq.shape[1]), bf),
            pltpu.VMEM((WINDOW + TOK_DEV, 2 * wk.shape[1]), bf),
            pltpu.VMEM((R, wo.shape[0]), bf),
            pltpu.VMEM((n + 1, COL_CHUNKS, R, D // COL_CHUNKS), bf),
            pltpu.VMEM((R, D), f32),
            dma((4,)),
            dma((REACH, 2)),
            dma((2, n, row_chunks)),
            dma((2, n, row_chunks)),
            dma((REACH, n)),
            dma((REACH, n)),
            dma((2, n, COL_CHUNKS)),
            dma((2, n, COL_CHUNKS)),
        ],
        compiler_params=pltpu.CompilerParams(
            collective_id=0, has_side_effects=True, vmem_limit_bytes=62 * 1024 * 1024
        ),
    )(act, gain, wq, wk, wv, wo, cache, post, cosine, sine)


PHASES = 4
CHIPS = 4
CORES = 2


def phased_kernel(
    act_ref, gain_ref, wq_hbm, wk_hbm, wv_hbm, wo_hbm, cache_hbm, post_ref, cos_ref, sin_ref,
    out_ref,
    w, wo, act_in, rows, q_buf, kv, att, att_x, slots, acc, stage,
    w_sem, cache_sem, spread_send, spread_recv, ag_send, ag_recv, core_send, core_recv,
    kv_send, kv_recv, att_send, att_recv, rs_send, rs_recv, out_send, out_recv,
):
    n = 4
    s = lax.axis_index("seq")
    z = lax.axis_index("head")
    c = s // CORES
    k = lax.rem(s, CORES)
    B, D = act_in.shape[1:]
    KW = wk_hbm.shape[1] // CORES
    QW = wq_hbm.shape[1] // CORES
    heads_kv = KW // HD
    group = QW // KW
    bf, f32 = jnp.bfloat16, jnp.float32
    near = z // 2
    inner = (z > 0) & (z < n - 1)
    outer = (z == 0) | (z == n - 1)

    def remote(src, dst, send, recv, chip, core, plane):
        return pltpu.make_async_remote_copy(
            src_ref=src, dst_ref=dst, send_sem=send, recv_sem=recv,
            device_id=(chip * CORES + core, plane), device_id_type=MESH,
        )

    def chip_at(d):
        return [c + 1 - 2 * lax.rem(c, 2), lax.rem(c + 2, CHIPS), CHIPS - 1 - c][d]

    weight_copies = [
        pltpu.make_async_copy(wk_hbm.at[:, pl.ds(pl.multiple_of(k * KW, KW), KW)], w.at[:, pl.ds(0, KW)], w_sem.at[0]),
        pltpu.make_async_copy(wv_hbm.at[:, pl.ds(pl.multiple_of(k * KW, KW), KW)], w.at[:, pl.ds(KW, KW)], w_sem.at[1]),
        pltpu.make_async_copy(wq_hbm.at[:, pl.ds(pl.multiple_of(k * QW, QW), QW)], w.at[:, pl.ds(2 * KW, QW)], w_sem.at[2]),
        pltpu.make_async_copy(wo_hbm, wo, w_sem.at[3]),
    ]
    cache_copies = [
        pltpu.make_async_copy(
            cache_hbm.at[i, :, :, :, :, pl.ds(pl.multiple_of(k * KW, KW), KW)],
            kv.at[pl.ds(0, 4), :, :, :, pl.ds(i * KW, KW)],
            cache_sem.at[i],
        )
        for i in range(2)
    ]

    barrier = pltpu.get_barrier_semaphore()

    def greet(chip, core, plane):
        pl.semaphore_signal(barrier, inc=1, device_id=(chip * CORES + core, plane), device_id_type=MESH)

    for d in range(3):
        greet(chip_at(d), k, z)
    greet(c, 1 - k, z)

    @pl.when(z > 0)
    def _():
        greet(c, k, z - 1)

    @pl.when(z < n - 1)
    def _():
        greet(c, k, z + 1)

    for x in weight_copies + cache_copies:
        x.start()
    pl.semaphore_wait(barrier, 4 + jnp.where(inner, 2, 1))

    def spread_copy(d):
        to = chip_at(d)
        return remote(
            act_ref.at[pl.ds(pl.multiple_of(to * B, B), B), :], act_in.at[c],
            spread_send.at[d], spread_recv.at[c], to, k, z,
        )

    def spread_wait(t):
        remote(act_in.at[t], act_in.at[t], spread_send.at[0], spread_recv.at[t], c, k, z).wait_recv()

    def row_block(t, core, zb):
        return rows.at[t, zb // 2, core, lax.rem(zb, 2)]

    def ag_copy(t, direction, zb):
        where = row_block(t, k, zb)
        to = jnp.minimum(z + 1, n - 1) if direction == 0 else jnp.maximum(z - 1, 0)
        return remote(where, where, ag_send.at[t, direction, zb], ag_recv.at[t, zb], c, k, to)

    def core_copy(t, zb, core):
        where = row_block(t, core, zb)
        return remote(where, where, core_send.at[t, zb], core_recv.at[t, zb], c, 1 - k, z)

    def normalize(t):
        @pl.when(t != c)
        def _():
            spread_wait(t)

        def piece(i, carry):
            r0 = pl.multiple_of(i * 16, 16)
            x = act_in[t, pl.ds(r0, 16), :].astype(f32)
            y = x * lax.rsqrt(jnp.mean(x * x, axis=-1, keepdims=True) + EPSILON) * gain_ref[...].reshape(1, D)
            rows[t, near, k, lax.rem(z, 2), pl.ds(r0, 16), :] = y.astype(bf)
            return carry
        lax.fori_loop(0, B // 16, piece, 0)

    def forward(t, zb, right, left):
        if right:
            @pl.when(z < n - 1)
            def _():
                ag_copy(t, 0, zb).start()
        if left:
            @pl.when(z > 0)
            def _():
                ag_copy(t, 1, zb).start()
        core_copy(t, zb, k).start()

    def hop(t, h):
        @pl.when(z - h >= 0)
        def _():
            ag_copy(t, 0, z - h).wait_recv()
            forward(t, z - h, True, False)

        @pl.when(z + h < n)
        def _():
            ag_copy(t, 1, z + h).wait_recv()
            forward(t, z + h, False, True)

    def kv_copy(t, half, core, d, chip):
        where = kv.at[4 + 2 * (2 * t + core) + half, :, chip]
        return remote(where, where, kv_send.at[t, half, core, d], kv_recv.at[t, half, core, d], chip_at(d), k, z)

    def project(t, half):
        for i in range(2):
            core_copy(t, 2 * half + i, 1 - k).wait_recv()
        cosine = cos_ref[t, half]
        sine = sin_ref[t, half]
        x = rows.at[t, half]

        def matmul(c0, width):
            return jnp.dot(
                x[...].reshape(4 * B, D), w[:, pl.ds(c0, width)], preferred_element_type=f32
            )

        def rope(u):
            return u * cosine + pltpu.roll(u, HD // 2, 1) * sine

        for part in range(2):
            u = matmul(part * KW, KW)
            for h in range(heads_kv):
                v = u[:, h * HD:(h + 1) * HD]
                v = (rope(v) if part == 0 else v).astype(bf)
                for core in range(2):
                    for zz in range(2):
                        r0 = (core * 2 + zz) * B
                        c0 = part * KW + h * HD
                        kv[4 + 2 * (2 * t + core) + half, zz, c, :, c0:c0 + HD] = v[r0:r0 + B]
        for d in range(3):
            for core in range(2):
                kv_copy(t, half, core, 2 - d, c).start()

        def queries(i, carry):
            c0 = pl.multiple_of(i * 256, 256)
            u = matmul(2 * KW + c0, 256)
            for h in range(256 // HD):
                v = (rope(u[:, h * HD:(h + 1) * HD]) * SCALAR ** (-0.5)).astype(bf)
                for core in range(2):
                    q_buf[t, half, core, :, pl.ds(pl.multiple_of(c0 + h * HD, HD), HD)] = v[core * 2 * B:(core + 1) * 2 * B]
            return carry
        lax.fori_loop(0, QW // 256, queries, 0)

    M = group * 2 * B
    row = lax.rem(lax.broadcasted_iota(jnp.int32, (M, 256), 0), 2 * B)
    place = (row // B) * (CHIPS * B) + lax.rem(row, B) + c * B
    later = lax.broadcasted_iota(jnp.int32, (M, 256), 1) > place
    spans = [(0, 1), (1, 3), (4, 1)]

    def attend(t, core, half, dst, dst_c0):
        u = 2 * (2 * t + core) + half
        for g in range(heads_kv):
            q = jnp.concatenate(
                [q_buf[t, half, core, :, (g * group + a) * HD:(g * group + a + 1) * HD] for a in range(group)], axis=0
            )
            scores = []
            for j, (o, wd) in enumerate(spans):
                key = kv[pl.ds(u + o, wd), :, :, :, g * HD:(g + 1) * HD].reshape(wd * 256, HD)
                sc = lax.dot_general(q, key, (((1,), (1,)), ((), ())), preferred_element_type=f32)
                if j == 0:
                    sc = jnp.where(later, sc, -jnp.inf)
                if j == 2:
                    sc = jnp.where(later, -jnp.inf, sc)
                scores.append(sc)
            m = functools.reduce(jnp.maximum, [jnp.max(x, axis=-1, keepdims=True) for x in scores])
            total = 0.0
            o_sum = 0.0
            for (o, wd), sc in zip(spans, scores):
                e = jnp.exp(sc - m)
                total = total + jnp.sum(e, axis=-1, keepdims=True)
                v = kv[pl.ds(u + o, wd), :, :, :, KW + g * HD:KW + (g + 1) * HD].reshape(wd * 256, HD)
                o_sum = o_sum + jnp.dot(e.astype(bf), v, preferred_element_type=f32)
            o_sum = (o_sum / total).astype(bf)
            for a in range(group):
                c0 = dst_c0 + (g * group + a) * HD
                dst[t, half, :, pl.ds(pl.multiple_of(c0, HD), HD)] = o_sum[a * 2 * B:(a + 1) * 2 * B]

    def attend_halves(t, core, dst, dst_c0):
        def one(half, carry):
            attend(t, core, half, dst, dst_c0)
            return carry
        lax.fori_loop(0, 2, one, 0)

    def att_copy(t, core):
        return remote(
            att_x.at[t], att.at[t, :, :, pl.ds(pl.multiple_of(core * QW, QW), QW)],
            att_send.at[t], att_recv.at[t], c, 1 - k, z,
        )

    TILE = 256

    def project_out(t):
        def one(i, carry):
            w0 = pl.multiple_of(i * TILE, TILE)
            p = jnp.dot(att[t].reshape(n * B, CORES * QW), wo[:, pl.ds(w0, TILE)], preferred_element_type=f32)
            acc[lax.rem(t, 2), :, :, pl.ds(w0, TILE)] = p.reshape(n, B, TILE)
            return carry
        lax.fori_loop(0, D // TILE, one, 0)

    def relay_block(r):
        low = z < 2
        if r == 0:
            return jnp.where(low, n - 1, 0)
        if r == 1:
            return jnp.where(low, n - 2, 1)
        return z + 1 - 2 * lax.rem(z, 2)

    def rs_copy(t, b):
        up = b > z
        to = jnp.where(up, z + 1, z - 1)
        slot = jnp.where(b == z - 1, n, b)
        return remote(slots.at[t, b], slots.at[t, slot], rs_send.at[t, b], rs_recv.at[t, slot], c, k, to)

    def rs_wait(t, slot):
        remote(slots.at[t, slot], slots.at[t, slot], rs_send.at[t, 0], rs_recv.at[t, slot], c, k, z).wait_recv()

    WIDE = 768

    def relay(t, r, incoming):
        b = relay_block(r)
        if incoming:
            rs_wait(t, b)

        def one(i, carry):
            c0 = pl.multiple_of(i * WIDE, WIDE)
            x = acc[lax.rem(t, 2), b, :, pl.ds(c0, WIDE)]
            if incoming:
                x = x + slots[t, b, :, pl.ds(c0, WIDE)].astype(f32)
            slots[t, b, :, pl.ds(c0, WIDE)] = x.astype(bf)
            return carry
        lax.fori_loop(0, D // WIDE, one, 0)
        rs_copy(t, b).start()

    def out_copy(t):
        return remote(
            stage.at[t], out_ref.at[pl.ds(pl.multiple_of(c * B, B), B), :], out_send.at[t], out_recv.at[c], t, k, z,
        )

    def finish(t):
        @pl.when(z > 0)
        def _():
            rs_wait(t, z)

        @pl.when(z < n - 1)
        def _():
            rs_wait(t, n)

        def piece(i, carry):
            r0 = pl.multiple_of(i * 16, 16)
            x = acc[lax.rem(t, 2), z, pl.ds(r0, 16), :]
            x = x + jnp.where(z > 0, slots[t, z, pl.ds(r0, 16), :].astype(f32), 0.0)
            x = x + jnp.where(z < n - 1, slots[t, n, pl.ds(r0, 16), :].astype(f32), 0.0)
            y = x * lax.rsqrt(jnp.mean(x * x, axis=-1, keepdims=True) + EPSILON) * post_ref[...].reshape(1, D)
            y = (act_in[t, pl.ds(r0, 16), :].astype(f32) + y).astype(bf)

            @pl.when(t == c)
            def _():
                out_ref[pl.ds(pl.multiple_of(c * B + r0, 16), 16), :] = y

            @pl.when(t != c)
            def _():
                stage[t, pl.ds(r0, 16), :] = y
            return carry
        lax.fori_loop(0, B // 16, piece, 0)

        @pl.when(t != c)
        def _():
            out_copy(t).start()

    def spread():
        for d in range(3):
            spread_copy(2 - d).start()

    @pl.when(c == 0)
    def _():
        spread()

    act_in[c] = act_ref[pl.ds(pl.multiple_of(c * B, B), B), :]
    normalize(0)
    forward(0, z, True, True)

    @pl.when(c != 0)
    def _():
        spread()

    for x in cache_copies + weight_copies:
        x.wait()

    def slot_step(t, carry):
        gathers = t < PHASES
        computes = (t >= 1) & (t <= PHASES)
        sums = t >= 2

        @pl.when(gathers)
        def _():
            hop(t, 1)

        @pl.when(computes)
        def _():
            project(t - 1, 1 - near)

        @pl.when(t + 1 < PHASES)
        def _():
            normalize(t + 1)
            forward(t + 1, z, True, True)

        @pl.when(gathers)
        def _():
            project(t, near)

        @pl.when(sums & inner)
        def _():
            relay(t - 2, 0, True)

        @pl.when(gathers)
        def _():
            hop(t, 2)

        @pl.when(computes)
        def _():
            for half in range(2):
                for core in range(2):
                    for d in range(3):
                        kv_copy(t - 1, half, core, d, chip_at(d)).wait_recv()
            attend_halves(t - 1, 1 - k, att_x, 0)
            att_copy(t - 1, k).start()

        @pl.when(sums & inner)
        def _():
            relay(t - 2, 1, True)

        @pl.when(computes)
        def _():
            attend_halves(t - 1, k, att, k * QW)
            att_copy(t - 1, 1 - k).wait_recv()
            project_out(t - 1)

            @pl.when(outer)
            def _():
                for r in range(3):
                    relay(t - 1, r, False)

        @pl.when(sums & inner)
        def _():
            relay(t - 2, 2, True)

        @pl.when(sums)
        def _():
            finish(t - 2)

        @pl.when(gathers)
        def _():
            hop(t, 3)
        return carry

    lax.fori_loop(0, PHASES + 2, slot_step, 0)

    for d in range(3):
        chip = chip_at(d)
        where = out_ref.at[pl.ds(pl.multiple_of(chip * B, B), B), :]
        remote(where, where, out_send.at[0], out_recv.at[chip], c, k, z).wait_recv()

    for d in range(3):
        spread_copy(d).wait_send()

    def drain(t, carry):
        def blocks(b, carry):
            @pl.when((b <= z) & (z < n - 1))
            def _():
                ag_copy(t, 0, b).wait_send()

            @pl.when((b >= z) & (z > 0))
            def _():
                ag_copy(t, 1, b).wait_send()

            core_copy(t, b, k).wait_send()

            @pl.when(b != z)
            def _():
                rs_copy(t, b).wait_send()
            return carry
        lax.fori_loop(0, n, blocks, 0)
        for half in range(2):
            for core in range(2):
                for d in range(3):
                    kv_copy(t, half, core, d, c).wait_send()
        att_copy(t, k).wait_send()

        @pl.when(t != c)
        def _():
            out_copy(t).wait_send()
        return carry
    lax.fori_loop(0, PHASES, drain, 0)


def phased_per_device(act, gain, wq, wk, wv, wo, cache, post):
    R, D = act.shape
    n = 4
    B = R // CHIPS
    c = lax.axis_index("seq") // CORES
    t, half, core, zz, i = jnp.meshgrid(*[jnp.arange(x, dtype=jnp.int32) for x in (PHASES, 2, 2, 2, B)], indexing="ij")
    positions = TOK_DEV * (2 * t + core) + R * (2 * half + zz) + B * c + i
    cosine, sine = rope_tables(positions.reshape(-1).astype(jnp.float32))
    cosine = cosine.reshape(PHASES, 2, 4 * B, HD)
    sine = sine.reshape(PHASES, 2, 4 * B, HD)
    bf, f32 = jnp.bfloat16, jnp.float32
    vmem = pl.BlockSpec(memory_space=pltpu.VMEM)
    hbm = pl.BlockSpec(memory_space=pl.ANY)
    dma = pltpu.SemaphoreType.DMA
    KW, QW = wk.shape[1] // CORES, wq.shape[1] // CORES
    cache = cache.reshape(2, 4, 2, CHIPS, B, wk.shape[1])
    return pl.pallas_call(
        phased_kernel,
        out_shape=jax.ShapeDtypeStruct((R, D), bf),
        in_specs=[vmem, vmem, hbm, hbm, hbm, hbm, hbm, vmem, vmem, vmem],
        out_specs=vmem,
        scratch_shapes=[
            pltpu.VMEM((D, 2 * KW + QW), bf),
            pltpu.VMEM(wo.shape, bf),
            pltpu.VMEM((PHASES, B, D), bf),
            pltpu.VMEM((PHASES, 2, CORES, 2, B, D), bf),
            pltpu.VMEM((PHASES, 2, CORES, 2 * B, QW), bf),
            pltpu.VMEM((4 + 4 * PHASES, 2, CHIPS, B, 2 * KW), bf),
            pltpu.VMEM((PHASES, 2, 2 * B, CORES * QW), bf),
            pltpu.VMEM((PHASES, 2, 2 * B, QW), bf),
            pltpu.VMEM((PHASES, n + 1, B, D), bf),
            pltpu.VMEM((2, n, B, D), f32),
            pltpu.VMEM((PHASES, B, D), bf),
            dma((4,)),
            dma((2,)),
            dma((3,)),
            dma((CHIPS,)),
            dma((PHASES, 2, n)),
            dma((PHASES, n)),
            dma((PHASES, n)),
            dma((PHASES, n)),
            dma((PHASES, 2, CORES, 3)),
            dma((PHASES, 2, CORES, 3)),
            dma((PHASES,)),
            dma((PHASES,)),
            dma((PHASES, n)),
            dma((PHASES, n + 1)),
            dma((PHASES,)),
            dma((CHIPS,)),
        ],
        compiler_params=pltpu.CompilerParams(
            collective_id=1, has_side_effects=True, vmem_limit_bytes=62 * 1024 * 1024
        ),
    )(act, gain, wq, wk, wv, wo, cache, post, cosine, sine)


def solution(mesh):
    if mesh.shape["head"] == 4 and mesh.shape["seq"] == CHIPS * CORES:
        body = phased_per_device
    else:
        body = functools.partial(per_device, mesh.shape["head"], mesh.shape["seq"])
    return jax.shard_map(
        body,
        mesh=mesh,
        in_specs=(
            P(("seq", "head"), None),
            P(),
            P(None, "head"),
            P(None, "head"),
            P(None, "head"),
            P("head", None),
            P(None, None, "head"),
            P(),
        ),
        out_specs=P(("seq", "head"), None),
        check_vma=False,
    )
```

```python
import functools
import jax
import jax.numpy as jnp
from jax import lax
from jax.experimental import pallas as pl
from jax.experimental.pallas import tpu as pltpu
from jax.sharding import PartitionSpec as P

HD = 128
WINDOW = 1024
SCALAR = 168
TOK_DEV = 512
EPSILON = 1e-06
ROPE_BASE = 10000.0
REACH = WINDOW // TOK_DEV
COL_CHUNKS = 7
MESH = pl.DeviceIdType.MESH


def rope_tables(positions):
    half_size = HD // 2
    frequency = ROPE_BASE ** (-(jnp.arange(half_size, dtype=jnp.float32) * 2.0 / HD))
    angles = positions[:, None] * frequency[None, :]
    cosine = jnp.cos(angles)
    sine = jnp.sin(angles)
    return jnp.concatenate([cosine, cosine], axis=1), jnp.concatenate([-sine, sine], axis=1)


def kernel(
    n, s_count,
    act_ref, gain_ref, wq_hbm, wk_hbm, wv_hbm, wo_hbm, cache_hbm, post_ref, cos_ref, sin_ref,
    out_ref,
    wq, wk, wv, wo, rows, q_buf, kv, att, slots, acc,
    w_sem, cache_sem, ag_send, ag_recv, kv_send, kv_recv, rs_send, rs_recv,
):
    s = lax.axis_index("seq")
    z = lax.axis_index("head")
    R, D = act_ref.shape
    kv_width = wk.shape[1]
    heads_kv = kv_width // HD
    group = wq.shape[1] // kv_width
    row_chunks = ag_send.shape[2]
    CR = R // row_chunks
    CD = D // COL_CHUNKS

    weight_copies = [
        pltpu.make_async_copy(src, dst, w_sem.at[i])
        for i, (src, dst) in enumerate([(wk_hbm, wk), (wv_hbm, wv), (wq_hbm, wq), (wo_hbm, wo)])
    ]
    for c in weight_copies:
        c.start()

    def cache_copies(d):
        return [
            pltpu.make_async_copy(
                cache_hbm.at[i, pl.ds(pl.multiple_of(WINDOW + (s - d) * TOK_DEV, TOK_DEV), TOK_DEV), :],
                kv.at[pl.ds(WINDOW - d * TOK_DEV, TOK_DEV), pl.ds(i * kv_width, kv_width)],
                cache_sem.at[d - 1, i],
            )
            for i in range(2)
        ]

    for d in range(1, REACH + 1):
        @pl.when(s < d)
        def _():
            for c in cache_copies(d):
                c.start()

    barrier = pltpu.get_barrier_semaphore()

    def greet(cond, ds, dz):
        @pl.when(cond)
        def _():
            pl.semaphore_signal(barrier, inc=1, device_id=(s + ds, z + dz), device_id_type=MESH)

    partners = [(z > 0, 0, -1), (z < n - 1, 0, 1)]
    for d in range(1, REACH + 1):
        partners += [(s >= d, -d, 0), (s + d < s_count, d, 0)]
    for p in partners:
        greet(*p)

    def norm_chunk(i, carry):
        r0 = pl.multiple_of(i * 16, 16)
        x = act_ref[pl.ds(r0, 16), :].astype(jnp.float32)
        y = x * lax.rsqrt(jnp.mean(x * x, axis=-1, keepdims=True) + EPSILON) * gain_ref[...].reshape(1, D)
        rows[z, pl.ds(r0, 16), :] = y.astype(jnp.bfloat16)
        return carry

    pl.semaphore_wait(barrier, sum(jnp.where(p[0], 1, 0) for p in partners))

    right = lax.rem(z + 1, n)
    left = lax.rem(z + n - 1, n)

    def ag_copy(direction, block, c):
        where = rows.at[block, pl.ds(c * CR, CR), :]
        return pltpu.make_async_remote_copy(
            src_ref=where, dst_ref=where,
            send_sem=ag_send.at[direction, block, c], recv_sem=ag_recv.at[direction, block, c],
            device_id=(s, right if direction == 0 else left), device_id_type=MESH,
        )

    def kv_copy(d, block):
        r0 = pl.multiple_of(block * R, R)
        return pltpu.make_async_remote_copy(
            src_ref=kv.at[pl.ds(WINDOW + r0, R), :],
            dst_ref=kv.at[pl.ds(WINDOW - d * TOK_DEV + r0, R), :],
            send_sem=kv_send.at[d - 1, block], recv_sem=kv_recv.at[d - 1, block],
            device_id=(lax.rem(s + d, s_count), z), device_id_type=MESH,
        )

    def rs_copy(direction, block, slot, c):
        where = slots.at[slot, c]
        return pltpu.make_async_remote_copy(
            src_ref=where, dst_ref=where,
            send_sem=rs_send.at[direction, block, c], recv_sem=rs_recv.at[direction, block, c],
            device_id=(s, right if direction == 0 else left), device_id_type=MESH,
        )

    def project(block):
        r0 = pl.multiple_of(block * R, R)
        cosine = cos_ref[pl.ds(r0, R), :]
        sine = sin_ref[pl.ds(r0, R), :]

        def run(w, tile, rotary, scale, dst, dst_r0, dst_c0):
            def one(i, carry):
                c0 = pl.multiple_of(i * tile, tile)
                t = jnp.dot(rows[block], w[:, pl.ds(c0, tile)], preferred_element_type=jnp.float32)
                for h in range(tile // HD):
                    u = t[:, h * HD:(h + 1) * HD]
                    if rotary:
                        u = u * cosine + pltpu.roll(u, HD // 2, 1) * sine
                    if scale is not None:
                        u = u * scale
                    dst[pl.ds(dst_r0, R), pl.ds(pl.multiple_of(dst_c0 + c0 + h * HD, HD), HD)] = u.astype(jnp.bfloat16)
                return carry
            lax.fori_loop(0, w.shape[1] // tile, one, 0)

        tile = min(256, kv_width)
        own = pl.multiple_of(WINDOW + r0, R)
        run(wk, tile, True, None, kv, own, 0)
        run(wv, tile, False, None, kv, own, kv_width)
        for d in range(1, REACH + 1):
            @pl.when(s + d < s_count)
            def _():
                kv_copy(d, block).start()
        run(wq, 256, True, SCALAR ** (-0.5), q_buf, r0, 0)

    for c in range(row_chunks):
        lax.fori_loop(c * CR // 16, (c + 1) * CR // 16, norm_chunk, 0)

        @pl.when(z < n - 1)
        def _():
            ag_copy(0, z, c).start()

        @pl.when(z > 0)
        def _():
            ag_copy(1, z, c).start()

    for i in range(3):
        weight_copies[i].wait()
    def gather_step(t, carry):
        from_left = z - t
        from_right = z + t
        for c in range(row_chunks):
            @pl.when(from_left >= 0)
            def _():
                ag_copy(0, from_left, c).wait_recv()

                @pl.when(z < n - 1)
                def _():
                    ag_copy(0, from_left, c).start()

            @pl.when(from_right < n)
            def _():
                ag_copy(1, from_right, c).wait_recv()

                @pl.when(z > 0)
                def _():
                    ag_copy(1, from_right, c).start()

            if c == 0:
                @pl.when(from_right - 1 < n)
                def _():
                    project(from_right - 1)

        @pl.when(from_left >= 0)
        def _():
            project(from_left)
        return carry

    lax.fori_loop(1, n, gather_step, 0)

    @pl.when(z == 0)
    def _():
        project(n - 1)

    for d in range(1, REACH + 1):
        @pl.when(s < d)
        def _():
            for c in cache_copies(d):
                c.wait()

        @pl.when(s >= d)
        def _():
            lax.fori_loop(0, n, lambda b, carry: (kv_copy(d, b).wait_recv(), carry)[1], 0)
    weight_copies[3].wait()

    row_i = lax.broadcasted_iota(jnp.int32, (group * R, R), 0)
    row_i = lax.rem(row_i, R)
    col_i = lax.broadcasted_iota(jnp.int32, (group * R, R), 1)
    later = col_i > row_i
    spans = [(0, R), (R, WINDOW - R), (WINDOW, R)]

    def attend(block):
        r0 = pl.multiple_of(block * R, R)
        for g in range(heads_kv):
            q = jnp.concatenate(
                [q_buf[pl.ds(r0, R), (g * group + a) * HD:(g * group + a + 1) * HD] for a in range(group)], axis=0
            )
            scores = []
            for j, (o, w) in enumerate(spans):
                k = kv[pl.ds(pl.multiple_of(r0 + o, R), w), g * HD:(g + 1) * HD]
                sc = lax.dot_general(q, k, (((1,), (1,)), ((), ())), preferred_element_type=jnp.float32)
                if j == 0:
                    sc = jnp.where(later, sc, -jnp.inf)
                if j == 2:
                    sc = jnp.where(later, -jnp.inf, sc)
                scores.append(sc)
            m = functools.reduce(jnp.maximum, [jnp.max(x, axis=-1, keepdims=True) for x in scores])
            total = 0.0
            o_sum = 0.0
            for (o, w), sc in zip(spans, scores):
                e = jnp.exp(sc - m)
                total = total + jnp.sum(e, axis=-1, keepdims=True)
                v = kv[pl.ds(pl.multiple_of(r0 + o, R), w), kv_width + g * HD:kv_width + (g + 1) * HD]
                o_sum = o_sum + jnp.dot(e.astype(jnp.bfloat16), v, preferred_element_type=jnp.float32)
            o_sum = (o_sum / total).astype(jnp.bfloat16)
            for a in range(group):
                att[:, (g * group + a) * HD:(g * group + a + 1) * HD] = o_sum[a * R:(a + 1) * R]

    TILE = 256

    def partial_out(direction, block, incoming):
        attend(block)
        for c in range(COL_CHUNKS):
            @pl.when(incoming)
            def _():
                rs_copy(direction, block, block, c).wait_recv()

            def one(i, carry):
                c0 = pl.multiple_of(i * TILE, TILE)
                w0 = pl.multiple_of(c * CD + i * TILE, TILE)
                p = jnp.dot(att[...], wo[:, pl.ds(w0, TILE)], preferred_element_type=jnp.float32)
                before = slots[block, c, :, pl.ds(c0, TILE)].astype(jnp.float32)
                p = p + jnp.where(incoming, before, 0.0)
                slots[block, c, :, pl.ds(c0, TILE)] = p.astype(jnp.bfloat16)
                return carry
            lax.fori_loop(0, CD // TILE, one, 0)
            send_out(direction, block, c).start()

    def send_out(direction, block, c):
        if direction == 0:
            return rs_copy(0, block, block, c)
        last = jnp.where(block == z - 1, n, block)
        return pltpu.make_async_remote_copy(
            src_ref=slots.at[block, c], dst_ref=slots.at[last, c],
            send_sem=rs_send.at[1, block, c], recv_sem=rs_recv.at[1, block, c],
            device_id=(s, left), device_id_type=MESH,
        )

    def scatter_step(t, carry):
        to_right = n - t
        to_left = t - 1

        @pl.when(to_right > z)
        def _():
            partial_out(0, to_right, z > 0)

        @pl.when(to_left < z)
        def _():
            partial_out(1, to_left, z < n - 1)
        return carry

    lax.fori_loop(1, n, scatter_step, 0)

    attend(z)

    def own(i, carry):
        w0 = pl.multiple_of(i * TILE, TILE)
        acc[:, pl.ds(w0, TILE)] = jnp.dot(att[...], wo[:, pl.ds(w0, TILE)], preferred_element_type=jnp.float32)
        return carry
    lax.fori_loop(0, D // TILE, own, 0)

    for c in range(COL_CHUNKS):
        for direction, slot, cond in ((0, z, z > 0), (1, n, z < n - 1)):
            @pl.when(cond)
            def _():
                rs_copy(direction, z, slot, c).wait_recv()
                acc[:, c * CD:(c + 1) * CD] += slots[slot, c].astype(jnp.float32)

    def finish(i, carry):
        r0 = pl.multiple_of(i * 16, 16)
        x = acc[pl.ds(r0, 16), :]
        y = x * lax.rsqrt(jnp.mean(x * x, axis=-1, keepdims=True) + EPSILON) * post_ref[...].reshape(1, D)
        out_ref[pl.ds(r0, 16), :] = (act_ref[pl.ds(r0, 16), :].astype(jnp.float32) + y).astype(jnp.bfloat16)
        return carry
    lax.fori_loop(0, R // 16, finish, 0)

    def drain(b, carry):
        @pl.when((b <= z) & (z < n - 1))
        def _():
            for c in range(row_chunks):
                ag_copy(0, b, c).wait_send()

        @pl.when((b >= z) & (z > 0))
        def _():
            for c in range(row_chunks):
                ag_copy(1, b, c).wait_send()

        @pl.when(b > z)
        def _():
            for c in range(COL_CHUNKS):
                send_out(0, b, c).wait_send()

        @pl.when(b < z)
        def _():
            for c in range(COL_CHUNKS):
                send_out(1, b, c).wait_send()

        for d in range(1, REACH + 1):
            @pl.when(s + d < s_count)
            def _():
                kv_copy(d, b).wait_send()
        return carry
    lax.fori_loop(0, n, drain, 0)


def per_device(n, s_count, act, gain, wq, wk, wv, wo, cache, post):
    R, D = act.shape
    row_chunks = min(4, R // 16)
    s = lax.axis_index("seq")
    positions = (s * TOK_DEV + jnp.arange(TOK_DEV, dtype=jnp.int32)).astype(jnp.float32)
    cosine, sine = rope_tables(positions)
    bf, f32 = jnp.bfloat16, jnp.float32
    vmem = pl.BlockSpec(memory_space=pltpu.VMEM)
    hbm = pl.BlockSpec(memory_space=pl.ANY)
    dma = pltpu.SemaphoreType.DMA
    return pl.pallas_call(
        functools.partial(kernel, n, s_count),
        out_shape=jax.ShapeDtypeStruct((R, D), bf),
        in_specs=[vmem, vmem, hbm, hbm, hbm, hbm, hbm, vmem, vmem, vmem],
        out_specs=vmem,
        scratch_shapes=[
            pltpu.VMEM(wq.shape, bf),
            pltpu.VMEM(wk.shape, bf),
            pltpu.VMEM(wv.shape, bf),
            pltpu.VMEM(wo.shape, bf),
            pltpu.VMEM((n, R, D), bf),
            pltpu.VMEM((TOK_DEV, wq.shape[1]), bf),
            pltpu.VMEM((WINDOW + TOK_DEV, 2 * wk.shape[1]), bf),
            pltpu.VMEM((R, wo.shape[0]), bf),
            pltpu.VMEM((n + 1, COL_CHUNKS, R, D // COL_CHUNKS), bf),
            pltpu.VMEM((R, D), f32),
            dma((4,)),
            dma((REACH, 2)),
            dma((2, n, row_chunks)),
            dma((2, n, row_chunks)),
            dma((REACH, n)),
            dma((REACH, n)),
            dma((2, n, COL_CHUNKS)),
            dma((2, n, COL_CHUNKS)),
        ],
        compiler_params=pltpu.CompilerParams(
            collective_id=0, has_side_effects=True, vmem_limit_bytes=62 * 1024 * 1024
        ),
    )(act, gain, wq, wk, wv, wo, cache, post, cosine, sine)


PHASES = 4
CHIPS = 4
CORES = 2


def phased_kernel(
    act_ref, gain_ref, wq_hbm, wk_hbm, wv_hbm, wo_hbm, cache_hbm, post_ref, cos_ref, sin_ref,
    out_ref,
    w, wo, act_in, rows, q_buf, kv, att, att_x, slots, acc, stage,
    w_sem, cache_sem, spread_send, spread_recv, ag_send, ag_recv, core_send, core_recv,
    kv_send, kv_recv, att_send, att_recv, rs_send, rs_recv, out_send, out_recv,
):
    n = 4
    s = lax.axis_index("seq")
    z = lax.axis_index("head")
    c = s // CORES
    k = lax.rem(s, CORES)
    B, D = act_in.shape[1:]
    KW = wk_hbm.shape[1] // CORES
    QW = wq_hbm.shape[1] // CORES
    heads_kv = KW // HD
    group = QW // KW
    bf, f32 = jnp.bfloat16, jnp.float32
    near = z // 2
    inner = (z > 0) & (z < n - 1)
    outer = (z == 0) | (z == n - 1)

    def remote(src, dst, send, recv, chip, core, plane):
        return pltpu.make_async_remote_copy(
            src_ref=src, dst_ref=dst, send_sem=send, recv_sem=recv,
            device_id=(chip * CORES + core, plane), device_id_type=MESH,
        )

    def chip_at(d):
        return [c + 1 - 2 * lax.rem(c, 2), lax.rem(c + 2, CHIPS), CHIPS - 1 - c][d]

    weight_copies = [
        pltpu.make_async_copy(wk_hbm.at[:, pl.ds(pl.multiple_of(k * KW, KW), KW)], w.at[:, pl.ds(0, KW)], w_sem.at[0]),
        pltpu.make_async_copy(wv_hbm.at[:, pl.ds(pl.multiple_of(k * KW, KW), KW)], w.at[:, pl.ds(KW, KW)], w_sem.at[1]),
        pltpu.make_async_copy(wq_hbm.at[:, pl.ds(pl.multiple_of(k * QW, QW), QW)], w.at[:, pl.ds(2 * KW, QW)], w_sem.at[2]),
        pltpu.make_async_copy(wo_hbm, wo, w_sem.at[3]),
    ]
    cache_copies = [
        pltpu.make_async_copy(
            cache_hbm.at[i, :, :, :, :, pl.ds(pl.multiple_of(k * KW, KW), KW)],
            kv.at[pl.ds(0, 4), :, :, :, pl.ds(i * KW, KW)],
            cache_sem.at[i],
        )
        for i in range(2)
    ]

    barrier = pltpu.get_barrier_semaphore()

    def greet(chip, core, plane):
        pl.semaphore_signal(barrier, inc=1, device_id=(chip * CORES + core, plane), device_id_type=MESH)

    for d in range(3):
        greet(chip_at(d), k, z)
    greet(c, 1 - k, z)

    @pl.when(z > 0)
    def _():
        greet(c, k, z - 1)

    @pl.when(z < n - 1)
    def _():
        greet(c, k, z + 1)

    for x in weight_copies + cache_copies:
        x.start()
    pl.semaphore_wait(barrier, 4 + jnp.where(inner, 2, 1))

    def spread_copy(d):
        to = chip_at(d)
        return remote(
            act_ref.at[pl.ds(pl.multiple_of(to * B, B), B), :], act_in.at[c],
            spread_send.at[d], spread_recv.at[c], to, k, z,
        )

    def spread_wait(t):
        remote(act_in.at[t], act_in.at[t], spread_send.at[0], spread_recv.at[t], c, k, z).wait_recv()

    def row_block(t, core, zb):
        return rows.at[t, zb // 2, core, lax.rem(zb, 2)]

    def ag_copy(t, direction, zb):
        where = row_block(t, k, zb)
        to = jnp.minimum(z + 1, n - 1) if direction == 0 else jnp.maximum(z - 1, 0)
        return remote(where, where, ag_send.at[t, direction, zb], ag_recv.at[t, zb], c, k, to)

    def core_copy(t, zb, core):
        where = row_block(t, core, zb)
        return remote(where, where, core_send.at[t, zb], core_recv.at[t, zb], c, 1 - k, z)

    def normalize(t):
        @pl.when(t != c)
        def _():
            spread_wait(t)

        def piece(i, carry):
            r0 = pl.multiple_of(i * 16, 16)
            x = act_in[t, pl.ds(r0, 16), :].astype(f32)
            y = x * lax.rsqrt(jnp.mean(x * x, axis=-1, keepdims=True) + EPSILON) * gain_ref[...].reshape(1, D)
            rows[t, near, k, lax.rem(z, 2), pl.ds(r0, 16), :] = y.astype(bf)
            return carry
        lax.fori_loop(0, B // 16, piece, 0)

    def forward(t, zb, right, left):
        if right:
            @pl.when(z < n - 1)
            def _():
                ag_copy(t, 0, zb).start()
        if left:
            @pl.when(z > 0)
            def _():
                ag_copy(t, 1, zb).start()
        core_copy(t, zb, k).start()

    def hop(t, h):
        @pl.when(z - h >= 0)
        def _():
            ag_copy(t, 0, z - h).wait_recv()
            forward(t, z - h, True, False)

        @pl.when(z + h < n)
        def _():
            ag_copy(t, 1, z + h).wait_recv()
            forward(t, z + h, False, True)

    def kv_copy(t, half, core, d, chip):
        where = kv.at[4 + 2 * (2 * t + core) + half, :, chip]
        return remote(where, where, kv_send.at[t, half, core, d], kv_recv.at[t, half, core, d], chip_at(d), k, z)

    def project(t, half):
        for i in range(2):
            core_copy(t, 2 * half + i, 1 - k).wait_recv()
        cosine = cos_ref[t, half]
        sine = sin_ref[t, half]
        x = rows.at[t, half]

        def matmul(c0, width):
            return jnp.dot(
                x[...].reshape(4 * B, D), w[:, pl.ds(c0, width)], preferred_element_type=f32
            )

        def rope(u):
            return u * cosine + pltpu.roll(u, HD // 2, 1) * sine

        for part in range(2):
            u = matmul(part * KW, KW)
            for h in range(heads_kv):
                v = u[:, h * HD:(h + 1) * HD]
                v = (rope(v) if part == 0 else v).astype(bf)
                for core in range(2):
                    for zz in range(2):
                        r0 = (core * 2 + zz) * B
                        c0 = part * KW + h * HD
                        kv[4 + 2 * (2 * t + core) + half, zz, c, :, c0:c0 + HD] = v[r0:r0 + B]

        def queries(i, carry):
            c0 = pl.multiple_of(i * 256, 256)
            u = matmul(2 * KW + c0, 256)
            for h in range(256 // HD):
                v = (rope(u[:, h * HD:(h + 1) * HD]) * SCALAR ** (-0.5)).astype(bf)
                for core in range(2):
                    q_buf[t, half, core, :, pl.ds(pl.multiple_of(c0 + h * HD, HD), HD)] = v[core * 2 * B:(core + 1) * 2 * B]
            return carry
        lax.fori_loop(0, QW // 256, queries, 0)

    def send_kv(t, half):
        for d in range(3):
            for core in range(2):
                kv_copy(t, half, core, 2 - d, c).start()

    M = group * 2 * B
    row = lax.rem(lax.broadcasted_iota(jnp.int32, (M, 256), 0), 2 * B)
    place = (row // B) * (CHIPS * B) + lax.rem(row, B) + c * B
    later = lax.broadcasted_iota(jnp.int32, (M, 256), 1) > place
    spans = [(0, 1), (1, 3), (4, 1)]

    def attend(t, core, half, dst, dst_c0):
        u = 2 * (2 * t + core) + half
        for g in range(heads_kv):
            q = jnp.concatenate(
                [q_buf[t, half, core, :, (g * group + a) * HD:(g * group + a + 1) * HD] for a in range(group)], axis=0
            )
            scores = []
            for j, (o, wd) in enumerate(spans):
                key = kv[pl.ds(u + o, wd), :, :, :, g * HD:(g + 1) * HD].reshape(wd * 256, HD)
                sc = lax.dot_general(q, key, (((1,), (1,)), ((), ())), preferred_element_type=f32)
                if j == 0:
                    sc = jnp.where(later, sc, -jnp.inf)
                if j == 2:
                    sc = jnp.where(later, -jnp.inf, sc)
                scores.append(sc)
            m = functools.reduce(jnp.maximum, [jnp.max(x, axis=-1, keepdims=True) for x in scores])
            total = 0.0
            o_sum = 0.0
            for (o, wd), sc in zip(spans, scores):
                e = jnp.exp(sc - m)
                total = total + jnp.sum(e, axis=-1, keepdims=True)
                v = kv[pl.ds(u + o, wd), :, :, :, KW + g * HD:KW + (g + 1) * HD].reshape(wd * 256, HD)
                o_sum = o_sum + jnp.dot(e.astype(bf), v, preferred_element_type=f32)
            o_sum = (o_sum / total).astype(bf)
            for a in range(group):
                c0 = dst_c0 + (g * group + a) * HD
                dst[t, half, :, pl.ds(pl.multiple_of(c0, HD), HD)] = o_sum[a * 2 * B:(a + 1) * 2 * B]

    def att_copy(t, half, core):
        return remote(
            att_x.at[t, half], att.at[t, half, :, pl.ds(pl.multiple_of(core * QW, QW), QW)],
            att_send.at[t, half], att_recv.at[t, half], c, 1 - k, z,
        )

    TILE = 256

    def attend_half(t, half):
        attend(t, 1 - k, half, att_x, 0)
        att_copy(t, half, k).start()
        attend(t, k, half, att, k * QW)
        att_copy(t, half, 1 - k).wait_recv()

        def one(i, carry):
            w0 = pl.multiple_of(i * TILE, TILE)
            p = jnp.dot(att[t, half], wo[:, pl.ds(w0, TILE)], preferred_element_type=f32)
            acc[lax.rem(t, 3), pl.ds(2 * half, 2), :, pl.ds(w0, TILE)] = p.reshape(2, B, TILE)
            return carry
        lax.fori_loop(0, D // TILE, one, 0)

    def relay_block(r):
        low = z < 2
        if r == 0:
            return jnp.where(low, n - 1, 0)
        if r == 1:
            return jnp.where(low, n - 2, 1)
        return z + 1 - 2 * lax.rem(z, 2)

    H = B // 2

    def rs_copy(t, b, piece):
        to = jnp.where(b > z, z + 1, z - 1)
        slot = jnp.where(b == z - 1, n, b)
        part = pl.ds(piece * H, H)
        return remote(
            slots.at[t, b, part, :], slots.at[t, slot, part, :],
            rs_send.at[t, b, piece], rs_recv.at[t, slot, piece], c, k, to,
        )

    def rs_wait(t, slot, piece):
        where = slots.at[t, slot, pl.ds(piece * H, H), :]
        remote(where, where, rs_send.at[t, 0, piece], rs_recv.at[t, slot, piece], c, k, z).wait_recv()

    WIDE = 1792

    def relay(t, r, incoming):
        b = relay_block(r)
        for piece in range(2):
            part = pl.ds(piece * H, H)
            if incoming:
                rs_wait(t, b, piece)

            def one(i, carry):
                c0 = pl.multiple_of(i * WIDE, WIDE)
                x = acc[lax.rem(t, 3), b, part, pl.ds(c0, WIDE)]
                if incoming:
                    x = x + slots[t, b, part, pl.ds(c0, WIDE)].astype(f32)
                slots[t, b, part, pl.ds(c0, WIDE)] = x.astype(bf)
                return carry
            lax.fori_loop(0, D // WIDE, one, 0)
            rs_copy(t, b, piece).start()

    def out_copy(t, piece):
        return remote(
            stage.at[t, pl.ds(piece * H, H), :],
            out_ref.at[pl.ds(pl.multiple_of(c * B + piece * H, H), H), :],
            out_send.at[t, piece], out_recv.at[c, piece], t, k, z,
        )

    def finish(t):
        for piece in range(2):
            @pl.when(z > 0)
            def _():
                rs_wait(t, z, piece)

            @pl.when(z < n - 1)
            def _():
                rs_wait(t, n, piece)

            part = pl.ds(piece * H, H)
            x = acc[lax.rem(t, 3), z, part, :]
            x = x + jnp.where(z > 0, slots[t, z, part, :].astype(f32), 0.0)
            x = x + jnp.where(z < n - 1, slots[t, n, part, :].astype(f32), 0.0)
            y = x * lax.rsqrt(jnp.mean(x * x, axis=-1, keepdims=True) + EPSILON) * post_ref[...].reshape(1, D)
            y = (act_in[t, part, :].astype(f32) + y).astype(bf)

            @pl.when(t == c)
            def _():
                out_ref[pl.ds(pl.multiple_of(c * B + piece * H, H), H), :] = y

            @pl.when(t != c)
            def _():
                stage[t, part, :] = y

            @pl.when(t != c)
            def _():
                out_copy(t, piece).start()

    def spread():
        for d in range(3):
            spread_copy(2 - d).start()

    @pl.when(c == 0)
    def _():
        spread()

    act_in[c] = act_ref[pl.ds(pl.multiple_of(c * B, B), B), :]
    normalize(c)
    forward(c, z, True, True)

    @pl.when(c != 0)
    def _():
        spread()
        normalize(0)
        forward(0, z, True, True)

    for x in cache_copies + weight_copies:
        x.wait()

    def own_rows(t):
        @pl.when(t != c)
        def _():
            normalize(t)
            forward(t, z, True, True)

    def slot_step(t, carry):
        gathers = t < PHASES
        computes = (t >= 1) & (t <= PHASES)
        sums = (t >= 2) & inner

        @pl.when(computes)
        def _():
            project(t - 1, 1 - near)
            send_kv(t - 1, 1 - near)

        @pl.when(gathers)
        def _():
            hop(t, 1)

        @pl.when((t >= 1) & (t + 1 < PHASES) & inner)
        def _():
            own_rows(t + 1)

        @pl.when(gathers)
        def _():
            project(t, near)

        @pl.when(t >= 3)
        def _():
            finish(t - 3)

        @pl.when(sums)
        def _():
            relay(t - 2, 0, True)

        @pl.when(computes)
        def _():
            for half in range(2):
                for core in range(2):
                    for d in range(3):
                        kv_copy(t - 1, half, core, d, chip_at(d)).wait_recv()

        @pl.when(gathers)
        def _():
            send_kv(t, near)

        @pl.when(t == 0)
        def _():
            def early(q, carry):
                @pl.when(outer | (q == 1))
                def _():
                    own_rows(q)
                return carry
            lax.fori_loop(1, PHASES, early, 0)

        @pl.when(computes)
        def _():
            attend_half(t - 1, 1 - near)

            @pl.when(outer)
            def _():
                for r in range(2):
                    relay(t - 1, r, False)

        @pl.when(gathers)
        def _():
            hop(t, 2)

        @pl.when(sums)
        def _():
            relay(t - 2, 1, True)

        @pl.when(computes)
        def _():
            attend_half(t - 1, near)

            @pl.when(outer)
            def _():
                relay(t - 1, 2, False)

        @pl.when(sums)
        def _():
            relay(t - 2, 2, True)

        @pl.when(gathers)
        def _():
            hop(t, 3)
        return carry

    lax.fori_loop(0, PHASES + 2, slot_step, 0)
    finish(PHASES - 1)

    for d in range(3):
        chip = chip_at(d)
        for piece in range(2):
            where = out_ref.at[pl.ds(pl.multiple_of(chip * B + piece * H, H), H), :]
            remote(where, where, out_send.at[0, piece], out_recv.at[chip, piece], c, k, z).wait_recv()

    for d in range(3):
        spread_copy(d).wait_send()

    def drain(t, carry):
        def blocks(b, carry):
            @pl.when((b <= z) & (z < n - 1))
            def _():
                ag_copy(t, 0, b).wait_send()

            @pl.when((b >= z) & (z > 0))
            def _():
                ag_copy(t, 1, b).wait_send()

            core_copy(t, b, k).wait_send()

            @pl.when(b != z)
            def _():
                for piece in range(2):
                    rs_copy(t, b, piece).wait_send()
            return carry
        lax.fori_loop(0, n, blocks, 0)
        for half in range(2):
            for core in range(2):
                for d in range(3):
                    kv_copy(t, half, core, d, c).wait_send()
        for half in range(2):
            att_copy(t, half, k).wait_send()

        @pl.when(t != c)
        def _():
            for piece in range(2):
                out_copy(t, piece).wait_send()
        return carry
    lax.fori_loop(0, PHASES, drain, 0)


def phased_per_device(act, gain, wq, wk, wv, wo, cache, post):
    R, D = act.shape
    n = 4
    B = R // CHIPS
    c = lax.axis_index("seq") // CORES
    t, half, core, zz, i = jnp.meshgrid(*[jnp.arange(x, dtype=jnp.int32) for x in (PHASES, 2, 2, 2, B)], indexing="ij")
    positions = TOK_DEV * (2 * t + core) + R * (2 * half + zz) + B * c + i
    cosine, sine = rope_tables(positions.reshape(-1).astype(jnp.float32))
    cosine = cosine.reshape(PHASES, 2, 4 * B, HD)
    sine = sine.reshape(PHASES, 2, 4 * B, HD)
    bf, f32 = jnp.bfloat16, jnp.float32
    vmem = pl.BlockSpec(memory_space=pltpu.VMEM)
    hbm = pl.BlockSpec(memory_space=pl.ANY)
    dma = pltpu.SemaphoreType.DMA
    KW, QW = wk.shape[1] // CORES, wq.shape[1] // CORES
    cache = cache.reshape(2, 4, 2, CHIPS, B, wk.shape[1])
    return pl.pallas_call(
        phased_kernel,
        out_shape=jax.ShapeDtypeStruct((R, D), bf),
        in_specs=[vmem, vmem, hbm, hbm, hbm, hbm, hbm, vmem, vmem, vmem],
        out_specs=vmem,
        scratch_shapes=[
            pltpu.VMEM((D, 2 * KW + QW), bf),
            pltpu.VMEM(wo.shape, bf),
            pltpu.VMEM((PHASES, B, D), bf),
            pltpu.VMEM((PHASES, 2, CORES, 2, B, D), bf),
            pltpu.VMEM((PHASES, 2, CORES, 2 * B, QW), bf),
            pltpu.VMEM((4 + 4 * PHASES, 2, CHIPS, B, 2 * KW), bf),
            pltpu.VMEM((PHASES, 2, 2 * B, CORES * QW), bf),
            pltpu.VMEM((PHASES, 2, 2 * B, QW), bf),
            pltpu.VMEM((PHASES, n + 1, B, D), bf),
            pltpu.VMEM((3, n, B, D), f32),
            pltpu.VMEM((PHASES, B, D), bf),
            dma((4,)),
            dma((2,)),
            dma((3,)),
            dma((CHIPS,)),
            dma((PHASES, 2, n)),
            dma((PHASES, n)),
            dma((PHASES, n)),
            dma((PHASES, n)),
            dma((PHASES, 2, CORES, 3)),
            dma((PHASES, 2, CORES, 3)),
            dma((PHASES, 2)),
            dma((PHASES, 2)),
            dma((PHASES, n, 2)),
            dma((PHASES, n + 1, 2)),
            dma((PHASES, 2)),
            dma((CHIPS, 2)),
        ],
        compiler_params=pltpu.CompilerParams(
            collective_id=1, has_side_effects=True, vmem_limit_bytes=62 * 1024 * 1024
        ),
    )(act, gain, wq, wk, wv, wo, cache, post, cosine, sine)


def solution(mesh):
    if mesh.shape["head"] == 4 and mesh.shape["seq"] == CHIPS * CORES:
        body = phased_per_device
    else:
        body = functools.partial(per_device, mesh.shape["head"], mesh.shape["seq"])
    return jax.shard_map(
        body,
        mesh=mesh,
        in_specs=(
            P(("seq", "head"), None),
            P(),
            P(None, "head"),
            P(None, "head"),
            P(None, "head"),
            P("head", None),
            P(None, None, "head"),
            P(),
        ),
        out_specs=P(("seq", "head"), None),
        check_vma=False,
    )
```

```python
import functools
import jax
import jax.numpy as jnp
from jax import lax
from jax.experimental import pallas as pl
from jax.experimental.pallas import tpu as pltpu
from jax.sharding import PartitionSpec as P

HD = 128
WINDOW = 1024
SCALAR = 168
TOK_DEV = 512
EPSILON = 1e-06
ROPE_BASE = 10000.0
REACH = WINDOW // TOK_DEV
COL_CHUNKS = 7
MESH = pl.DeviceIdType.MESH


def rope_tables(positions):
    half_size = HD // 2
    frequency = ROPE_BASE ** (-(jnp.arange(half_size, dtype=jnp.float32) * 2.0 / HD))
    angles = positions[:, None] * frequency[None, :]
    cosine = jnp.cos(angles)
    sine = jnp.sin(angles)
    return jnp.concatenate([cosine, cosine], axis=1), jnp.concatenate([-sine, sine], axis=1)


def kernel(
    n, s_count,
    act_ref, gain_ref, wq_hbm, wk_hbm, wv_hbm, wo_hbm, cache_hbm, post_ref, cos_ref, sin_ref,
    out_ref,
    wq, wk, wv, wo, rows, q_buf, kv, att, slots, acc,
    w_sem, cache_sem, ag_send, ag_recv, kv_send, kv_recv, rs_send, rs_recv,
):
    s = lax.axis_index("seq")
    z = lax.axis_index("head")
    R, D = act_ref.shape
    kv_width = wk.shape[1]
    heads_kv = kv_width // HD
    group = wq.shape[1] // kv_width
    row_chunks = ag_send.shape[2]
    CR = R // row_chunks
    CD = D // COL_CHUNKS

    weight_copies = [
        pltpu.make_async_copy(src, dst, w_sem.at[i])
        for i, (src, dst) in enumerate([(wk_hbm, wk), (wv_hbm, wv), (wq_hbm, wq), (wo_hbm, wo)])
    ]
    for c in weight_copies:
        c.start()

    def cache_copies(d):
        return [
            pltpu.make_async_copy(
                cache_hbm.at[i, pl.ds(pl.multiple_of(WINDOW + (s - d) * TOK_DEV, TOK_DEV), TOK_DEV), :],
                kv.at[pl.ds(WINDOW - d * TOK_DEV, TOK_DEV), pl.ds(i * kv_width, kv_width)],
                cache_sem.at[d - 1, i],
            )
            for i in range(2)
        ]

    for d in range(1, REACH + 1):
        @pl.when(s < d)
        def _():
            for c in cache_copies(d):
                c.start()

    barrier = pltpu.get_barrier_semaphore()

    def greet(cond, ds, dz):
        @pl.when(cond)
        def _():
            pl.semaphore_signal(barrier, inc=1, device_id=(s + ds, z + dz), device_id_type=MESH)

    partners = [(z > 0, 0, -1), (z < n - 1, 0, 1)]
    for d in range(1, REACH + 1):
        partners += [(s >= d, -d, 0), (s + d < s_count, d, 0)]
    for p in partners:
        greet(*p)

    def norm_chunk(i, carry):
        r0 = pl.multiple_of(i * 16, 16)
        x = act_ref[pl.ds(r0, 16), :].astype(jnp.float32)
        y = x * lax.rsqrt(jnp.mean(x * x, axis=-1, keepdims=True) + EPSILON) * gain_ref[...].reshape(1, D)
        rows[z, pl.ds(r0, 16), :] = y.astype(jnp.bfloat16)
        return carry

    pl.semaphore_wait(barrier, sum(jnp.where(p[0], 1, 0) for p in partners))

    right = lax.rem(z + 1, n)
    left = lax.rem(z + n - 1, n)

    def ag_copy(direction, block, c):
        where = rows.at[block, pl.ds(c * CR, CR), :]
        return pltpu.make_async_remote_copy(
            src_ref=where, dst_ref=where,
            send_sem=ag_send.at[direction, block, c], recv_sem=ag_recv.at[direction, block, c],
            device_id=(s, right if direction == 0 else left), device_id_type=MESH,
        )

    def kv_copy(d, block):
        r0 = pl.multiple_of(block * R, R)
        return pltpu.make_async_remote_copy(
            src_ref=kv.at[pl.ds(WINDOW + r0, R), :],
            dst_ref=kv.at[pl.ds(WINDOW - d * TOK_DEV + r0, R), :],
            send_sem=kv_send.at[d - 1, block], recv_sem=kv_recv.at[d - 1, block],
            device_id=(lax.rem(s + d, s_count), z), device_id_type=MESH,
        )

    def rs_copy(direction, block, slot, c):
        where = slots.at[slot, c]
        return pltpu.make_async_remote_copy(
            src_ref=where, dst_ref=where,
            send_sem=rs_send.at[direction, block, c], recv_sem=rs_recv.at[direction, block, c],
            device_id=(s, right if direction == 0 else left), device_id_type=MESH,
        )

    def project(block):
        r0 = pl.multiple_of(block * R, R)
        cosine = cos_ref[pl.ds(r0, R), :]
        sine = sin_ref[pl.ds(r0, R), :]

        def run(w, tile, rotary, scale, dst, dst_r0, dst_c0):
            def one(i, carry):
                c0 = pl.multiple_of(i * tile, tile)
                t = jnp.dot(rows[block], w[:, pl.ds(c0, tile)], preferred_element_type=jnp.float32)
                for h in range(tile // HD):
                    u = t[:, h * HD:(h + 1) * HD]
                    if rotary:
                        u = u * cosine + pltpu.roll(u, HD // 2, 1) * sine
                    if scale is not None:
                        u = u * scale
                    dst[pl.ds(dst_r0, R), pl.ds(pl.multiple_of(dst_c0 + c0 + h * HD, HD), HD)] = u.astype(jnp.bfloat16)
                return carry
            lax.fori_loop(0, w.shape[1] // tile, one, 0)

        tile = min(256, kv_width)
        own = pl.multiple_of(WINDOW + r0, R)
        run(wk, tile, True, None, kv, own, 0)
        run(wv, tile, False, None, kv, own, kv_width)
        for d in range(1, REACH + 1):
            @pl.when(s + d < s_count)
            def _():
                kv_copy(d, block).start()
        run(wq, 256, True, SCALAR ** (-0.5), q_buf, r0, 0)

    for c in range(row_chunks):
        lax.fori_loop(c * CR // 16, (c + 1) * CR // 16, norm_chunk, 0)

        @pl.when(z < n - 1)
        def _():
            ag_copy(0, z, c).start()

        @pl.when(z > 0)
        def _():
            ag_copy(1, z, c).start()

    for i in range(3):
        weight_copies[i].wait()
    def gather_step(t, carry):
        from_left = z - t
        from_right = z + t
        for c in range(row_chunks):
            @pl.when(from_left >= 0)
            def _():
                ag_copy(0, from_left, c).wait_recv()

                @pl.when(z < n - 1)
                def _():
                    ag_copy(0, from_left, c).start()

            @pl.when(from_right < n)
            def _():
                ag_copy(1, from_right, c).wait_recv()

                @pl.when(z > 0)
                def _():
                    ag_copy(1, from_right, c).start()

            if c == 0:
                @pl.when(from_right - 1 < n)
                def _():
                    project(from_right - 1)

        @pl.when(from_left >= 0)
        def _():
            project(from_left)
        return carry

    lax.fori_loop(1, n, gather_step, 0)

    @pl.when(z == 0)
    def _():
        project(n - 1)

    for d in range(1, REACH + 1):
        @pl.when(s < d)
        def _():
            for c in cache_copies(d):
                c.wait()

        @pl.when(s >= d)
        def _():
            lax.fori_loop(0, n, lambda b, carry: (kv_copy(d, b).wait_recv(), carry)[1], 0)
    weight_copies[3].wait()

    row_i = lax.broadcasted_iota(jnp.int32, (group * R, R), 0)
    row_i = lax.rem(row_i, R)
    col_i = lax.broadcasted_iota(jnp.int32, (group * R, R), 1)
    later = col_i > row_i
    spans = [(0, R), (R, WINDOW - R), (WINDOW, R)]

    def attend(block):
        r0 = pl.multiple_of(block * R, R)
        for g in range(heads_kv):
            q = jnp.concatenate(
                [q_buf[pl.ds(r0, R), (g * group + a) * HD:(g * group + a + 1) * HD] for a in range(group)], axis=0
            )
            scores = []
            for j, (o, w) in enumerate(spans):
                k = kv[pl.ds(pl.multiple_of(r0 + o, R), w), g * HD:(g + 1) * HD]
                sc = lax.dot_general(q, k, (((1,), (1,)), ((), ())), preferred_element_type=jnp.float32)
                if j == 0:
                    sc = jnp.where(later, sc, -jnp.inf)
                if j == 2:
                    sc = jnp.where(later, -jnp.inf, sc)
                scores.append(sc)
            m = functools.reduce(jnp.maximum, [jnp.max(x, axis=-1, keepdims=True) for x in scores])
            total = 0.0
            o_sum = 0.0
            for (o, w), sc in zip(spans, scores):
                e = jnp.exp(sc - m)
                total = total + jnp.sum(e, axis=-1, keepdims=True)
                v = kv[pl.ds(pl.multiple_of(r0 + o, R), w), kv_width + g * HD:kv_width + (g + 1) * HD]
                o_sum = o_sum + jnp.dot(e.astype(jnp.bfloat16), v, preferred_element_type=jnp.float32)
            o_sum = (o_sum / total).astype(jnp.bfloat16)
            for a in range(group):
                att[:, (g * group + a) * HD:(g * group + a + 1) * HD] = o_sum[a * R:(a + 1) * R]

    TILE = 256

    def partial_out(direction, block, incoming):
        attend(block)
        for c in range(COL_CHUNKS):
            @pl.when(incoming)
            def _():
                rs_copy(direction, block, block, c).wait_recv()

            def one(i, carry):
                c0 = pl.multiple_of(i * TILE, TILE)
                w0 = pl.multiple_of(c * CD + i * TILE, TILE)
                p = jnp.dot(att[...], wo[:, pl.ds(w0, TILE)], preferred_element_type=jnp.float32)
                before = slots[block, c, :, pl.ds(c0, TILE)].astype(jnp.float32)
                p = p + jnp.where(incoming, before, 0.0)
                slots[block, c, :, pl.ds(c0, TILE)] = p.astype(jnp.bfloat16)
                return carry
            lax.fori_loop(0, CD // TILE, one, 0)
            send_out(direction, block, c).start()

    def send_out(direction, block, c):
        if direction == 0:
            return rs_copy(0, block, block, c)
        last = jnp.where(block == z - 1, n, block)
        return pltpu.make_async_remote_copy(
            src_ref=slots.at[block, c], dst_ref=slots.at[last, c],
            send_sem=rs_send.at[1, block, c], recv_sem=rs_recv.at[1, block, c],
            device_id=(s, left), device_id_type=MESH,
        )

    def scatter_step(t, carry):
        to_right = n - t
        to_left = t - 1

        @pl.when(to_right > z)
        def _():
            partial_out(0, to_right, z > 0)

        @pl.when(to_left < z)
        def _():
            partial_out(1, to_left, z < n - 1)
        return carry

    lax.fori_loop(1, n, scatter_step, 0)

    attend(z)

    def own(i, carry):
        w0 = pl.multiple_of(i * TILE, TILE)
        acc[:, pl.ds(w0, TILE)] = jnp.dot(att[...], wo[:, pl.ds(w0, TILE)], preferred_element_type=jnp.float32)
        return carry
    lax.fori_loop(0, D // TILE, own, 0)

    for c in range(COL_CHUNKS):
        for direction, slot, cond in ((0, z, z > 0), (1, n, z < n - 1)):
            @pl.when(cond)
            def _():
                rs_copy(direction, z, slot, c).wait_recv()
                acc[:, c * CD:(c + 1) * CD] += slots[slot, c].astype(jnp.float32)

    def finish(i, carry):
        r0 = pl.multiple_of(i * 16, 16)
        x = acc[pl.ds(r0, 16), :]
        y = x * lax.rsqrt(jnp.mean(x * x, axis=-1, keepdims=True) + EPSILON) * post_ref[...].reshape(1, D)
        out_ref[pl.ds(r0, 16), :] = (act_ref[pl.ds(r0, 16), :].astype(jnp.float32) + y).astype(jnp.bfloat16)
        return carry
    lax.fori_loop(0, R // 16, finish, 0)

    def drain(b, carry):
        @pl.when((b <= z) & (z < n - 1))
        def _():
            for c in range(row_chunks):
                ag_copy(0, b, c).wait_send()

        @pl.when((b >= z) & (z > 0))
        def _():
            for c in range(row_chunks):
                ag_copy(1, b, c).wait_send()

        @pl.when(b > z)
        def _():
            for c in range(COL_CHUNKS):
                send_out(0, b, c).wait_send()

        @pl.when(b < z)
        def _():
            for c in range(COL_CHUNKS):
                send_out(1, b, c).wait_send()

        for d in range(1, REACH + 1):
            @pl.when(s + d < s_count)
            def _():
                kv_copy(d, b).wait_send()
        return carry
    lax.fori_loop(0, n, drain, 0)


def per_device(n, s_count, act, gain, wq, wk, wv, wo, cache, post):
    R, D = act.shape
    row_chunks = min(4, R // 16)
    s = lax.axis_index("seq")
    positions = (s * TOK_DEV + jnp.arange(TOK_DEV, dtype=jnp.int32)).astype(jnp.float32)
    cosine, sine = rope_tables(positions)
    bf, f32 = jnp.bfloat16, jnp.float32
    vmem = pl.BlockSpec(memory_space=pltpu.VMEM)
    hbm = pl.BlockSpec(memory_space=pl.ANY)
    dma = pltpu.SemaphoreType.DMA
    return pl.pallas_call(
        functools.partial(kernel, n, s_count),
        out_shape=jax.ShapeDtypeStruct((R, D), bf),
        in_specs=[vmem, vmem, hbm, hbm, hbm, hbm, hbm, vmem, vmem, vmem],
        out_specs=vmem,
        scratch_shapes=[
            pltpu.VMEM(wq.shape, bf),
            pltpu.VMEM(wk.shape, bf),
            pltpu.VMEM(wv.shape, bf),
            pltpu.VMEM(wo.shape, bf),
            pltpu.VMEM((n, R, D), bf),
            pltpu.VMEM((TOK_DEV, wq.shape[1]), bf),
            pltpu.VMEM((WINDOW + TOK_DEV, 2 * wk.shape[1]), bf),
            pltpu.VMEM((R, wo.shape[0]), bf),
            pltpu.VMEM((n + 1, COL_CHUNKS, R, D // COL_CHUNKS), bf),
            pltpu.VMEM((R, D), f32),
            dma((4,)),
            dma((REACH, 2)),
            dma((2, n, row_chunks)),
            dma((2, n, row_chunks)),
            dma((REACH, n)),
            dma((REACH, n)),
            dma((2, n, COL_CHUNKS)),
            dma((2, n, COL_CHUNKS)),
        ],
        compiler_params=pltpu.CompilerParams(
            collective_id=0, has_side_effects=True, vmem_limit_bytes=62 * 1024 * 1024
        ),
    )(act, gain, wq, wk, wv, wo, cache, post, cosine, sine)


PHASES = 4
CHIPS = 4
CORES = 2


def phased_kernel(
    act_ref, gain_ref, wq_hbm, wk_hbm, wv_hbm, wo_hbm, cache_hbm, post_ref, far_cos, far_sin, low_cos, low_sin,
    out_ref,
    w, wo, act_in, rows, q_buf, kv, att, att_x, slots, acc, stage,
    w_sem, cache_sem, spread_send, spread_recv, ag_send, ag_recv, core_send, core_recv,
    kv_send, kv_recv, att_send, att_recv, rs_send, rs_recv, out_send, out_recv,
):
    n = 4
    s = lax.axis_index("seq")
    z = lax.axis_index("head")
    c = s // CORES
    k = lax.rem(s, CORES)
    B, D = act_in.shape[1:]
    KW = wk_hbm.shape[1] // CORES
    QW = wq_hbm.shape[1] // CORES
    heads_kv = KW // HD
    group = QW // KW
    bf, f32 = jnp.bfloat16, jnp.float32
    near = z // 2
    inner = (z > 0) & (z < n - 1)
    outer = (z == 0) | (z == n - 1)

    def remote(src, dst, send, recv, chip, core, plane):
        return pltpu.make_async_remote_copy(
            src_ref=src, dst_ref=dst, send_sem=send, recv_sem=recv,
            device_id=(chip * CORES + core, plane), device_id_type=MESH,
        )

    def chip_at(d):
        return [c + 1 - 2 * lax.rem(c, 2), lax.rem(c + 2, CHIPS), CHIPS - 1 - c][d]

    weight_copies = [
        pltpu.make_async_copy(wk_hbm.at[:, pl.ds(pl.multiple_of(k * KW, KW), KW)], w.at[:, pl.ds(0, KW)], w_sem.at[0]),
        pltpu.make_async_copy(wv_hbm.at[:, pl.ds(pl.multiple_of(k * KW, KW), KW)], w.at[:, pl.ds(KW, KW)], w_sem.at[1]),
        pltpu.make_async_copy(wq_hbm.at[:, pl.ds(pl.multiple_of(k * QW, QW), QW)], w.at[:, pl.ds(2 * KW, QW)], w_sem.at[2]),
        pltpu.make_async_copy(wo_hbm, wo, w_sem.at[3]),
    ]
    cache_copies = [
        pltpu.make_async_copy(
            cache_hbm.at[i, :, :, :, :, pl.ds(pl.multiple_of(k * KW, KW), KW)],
            kv.at[pl.ds(0, 4), :, :, :, pl.ds(i * KW, KW)],
            cache_sem.at[i],
        )
        for i in range(2)
    ]

    barrier = pltpu.get_barrier_semaphore()

    def greet(chip, core, plane):
        pl.semaphore_signal(barrier, inc=1, device_id=(chip * CORES + core, plane), device_id_type=MESH)

    for d in range(3):
        greet(chip_at(d), k, z)
    greet(c, 1 - k, z)

    @pl.when(z > 0)
    def _():
        greet(c, k, z - 1)

    @pl.when(z < n - 1)
    def _():
        greet(c, k, z + 1)

    for x in weight_copies + cache_copies:
        x.start()
    pl.semaphore_wait(barrier, 4 + jnp.where(inner, 2, 1))

    def spread_copy(d):
        to = chip_at(d)
        return remote(
            act_ref.at[pl.ds(pl.multiple_of(to * B, B), B), :], act_in.at[c],
            spread_send.at[d], spread_recv.at[c], to, k, z,
        )

    def spread_wait(t):
        remote(act_in.at[t], act_in.at[t], spread_send.at[0], spread_recv.at[t], c, k, z).wait_recv()

    def row_block(t, core, zb):
        return rows.at[t, zb // 2, core, lax.rem(zb, 2)]

    def ag_copy(t, direction, zb):
        where = row_block(t, k, zb)
        to = jnp.minimum(z + 1, n - 1) if direction == 0 else jnp.maximum(z - 1, 0)
        return remote(where, where, ag_send.at[t, direction, zb], ag_recv.at[t, zb], c, k, to)

    def core_copy(t, zb, core):
        where = row_block(t, core, zb)
        return remote(where, where, core_send.at[t, zb], core_recv.at[t, zb], c, 1 - k, z)

    def normalize(t):
        @pl.when(t != c)
        def _():
            spread_wait(t)

        def piece(i, carry):
            r0 = pl.multiple_of(i * 16, 16)
            x = act_in[t, pl.ds(r0, 16), :].astype(f32)
            y = x * lax.rsqrt(jnp.mean(x * x, axis=-1, keepdims=True) + EPSILON) * gain_ref[...].reshape(1, D)
            rows[t, near, k, lax.rem(z, 2), pl.ds(r0, 16), :] = y.astype(bf)
            return carry
        lax.fori_loop(0, B // 16, piece, 0)

    def forward(t, zb, right, left):
        if right:
            @pl.when(z < n - 1)
            def _():
                ag_copy(t, 0, zb).start()
        if left:
            @pl.when(z > 0)
            def _():
                ag_copy(t, 1, zb).start()
        core_copy(t, zb, k).start()

    def hop(t, h):
        @pl.when(z - h >= 0)
        def _():
            ag_copy(t, 0, z - h).wait_recv()
            forward(t, z - h, True, False)

        @pl.when(z + h < n)
        def _():
            ag_copy(t, 1, z + h).wait_recv()
            forward(t, z + h, False, True)

    def kv_copy(t, half, core, d, chip):
        where = kv.at[4 + 2 * (2 * t + core) + half, :, chip]
        return remote(where, where, kv_send.at[t, half, core, d], kv_recv.at[t, half, core, d], chip_at(d), k, z)

    def project(t, half):
        for i in range(2):
            core_copy(t, 2 * half + i, 1 - k).wait_recv()
        table = 4 * (2 * t + half)
        cosine, sine = [], []
        for i in range(4):
            ca, sa = far_cos[table + i], far_sin[table + i]
            cb, sb = low_cos[...], low_sin[...]
            cosine.append(ca * cb - sa * sb)
            sine.append(sa * cb + ca * sb)
        cosine = jnp.concatenate(cosine, axis=0)
        sine = jnp.concatenate(sine, axis=0)
        x = rows.at[t, half]

        def matmul(c0, width):
            return jnp.dot(
                x[...].reshape(4 * B, D), w[:, pl.ds(c0, width)], preferred_element_type=f32
            )

        def rope(u):
            return u * cosine + pltpu.roll(u, HD // 2, 1) * sine

        for part in range(2):
            u = matmul(part * KW, KW)
            for h in range(heads_kv):
                v = u[:, h * HD:(h + 1) * HD]
                v = (rope(v) if part == 0 else v).astype(bf)
                for core in range(2):
                    for zz in range(2):
                        r0 = (core * 2 + zz) * B
                        c0 = part * KW + h * HD
                        kv[4 + 2 * (2 * t + core) + half, zz, c, :, c0:c0 + HD] = v[r0:r0 + B]

        def queries(i, carry):
            c0 = pl.multiple_of(i * 256, 256)
            u = matmul(2 * KW + c0, 256)
            for h in range(256 // HD):
                v = (rope(u[:, h * HD:(h + 1) * HD]) * SCALAR ** (-0.5)).astype(bf)
                for core in range(2):
                    q_buf[t, half, core, :, pl.ds(pl.multiple_of(c0 + h * HD, HD), HD)] = v[core * 2 * B:(core + 1) * 2 * B]
            return carry
        lax.fori_loop(0, QW // 256, queries, 0)

    def send_kv(t, half):
        for d in range(3):
            for core in range(2):
                kv_copy(t, half, core, 2 - d, c).start()

    M = group * 2 * B
    row = lax.rem(lax.broadcasted_iota(jnp.int32, (M, 256), 0), 2 * B)
    place = (row // B) * (CHIPS * B) + lax.rem(row, B) + c * B
    later = lax.broadcasted_iota(jnp.int32, (M, 256), 1) > place
    spans = [(0, 1), (1, 3), (4, 1)]

    def attend(t, core, half, dst, dst_c0):
        u = 2 * (2 * t + core) + half
        for g in range(heads_kv):
            q = jnp.concatenate(
                [q_buf[t, half, core, :, (g * group + a) * HD:(g * group + a + 1) * HD] for a in range(group)], axis=0
            )
            scores = []
            for j, (o, wd) in enumerate(spans):
                key = kv[pl.ds(u + o, wd), :, :, :, g * HD:(g + 1) * HD].reshape(wd * 256, HD)
                sc = lax.dot_general(q, key, (((1,), (1,)), ((), ())), preferred_element_type=f32)
                if j == 0:
                    sc = jnp.where(later, sc, -jnp.inf)
                if j == 2:
                    sc = jnp.where(later, -jnp.inf, sc)
                scores.append(sc)
            m = functools.reduce(jnp.maximum, [jnp.max(x, axis=-1, keepdims=True) for x in scores])
            total = 0.0
            o_sum = 0.0
            for (o, wd), sc in zip(spans, scores):
                e = jnp.exp(sc - m)
                total = total + jnp.sum(e, axis=-1, keepdims=True)
                v = kv[pl.ds(u + o, wd), :, :, :, KW + g * HD:KW + (g + 1) * HD].reshape(wd * 256, HD)
                o_sum = o_sum + jnp.dot(e.astype(bf), v, preferred_element_type=f32)
            o_sum = (o_sum / total).astype(bf)
            for a in range(group):
                c0 = dst_c0 + (g * group + a) * HD
                dst[t, half, :, pl.ds(pl.multiple_of(c0, HD), HD)] = o_sum[a * 2 * B:(a + 1) * 2 * B]

    def att_copy(t, half, core):
        return remote(
            att_x.at[t, half], att.at[t, half, :, pl.ds(pl.multiple_of(core * QW, QW), QW)],
            att_send.at[t, half], att_recv.at[t, half], c, 1 - k, z,
        )

    TILE = 1792

    def attend_half(t, half):
        attend(t, 1 - k, half, att_x, 0)
        att_copy(t, half, k).start()
        attend(t, k, half, att, k * QW)
        att_copy(t, half, 1 - k).wait_recv()

        def one(i, carry):
            w0 = pl.multiple_of(i * TILE, TILE)
            p = jnp.dot(att[t, half], wo[:, pl.ds(w0, TILE)], preferred_element_type=f32)
            acc[lax.rem(t, 3), pl.ds(2 * half, 2), :, pl.ds(w0, TILE)] = p.reshape(2, B, TILE)
            return carry
        lax.fori_loop(0, D // TILE, one, 0)

    def relay_block(r):
        low = z < 2
        if r == 0:
            return jnp.where(low, n - 1, 0)
        if r == 1:
            return jnp.where(low, n - 2, 1)
        return z + 1 - 2 * lax.rem(z, 2)

    H = B // 2

    def rs_copy(t, b, piece):
        to = jnp.where(b > z, z + 1, z - 1)
        slot = jnp.where(b == z - 1, n, b)
        part = pl.ds(piece * H, H)
        return remote(
            slots.at[t, b, part, :], slots.at[t, slot, part, :],
            rs_send.at[t, b, piece], rs_recv.at[t, slot, piece], c, k, to,
        )

    def rs_wait(t, slot, piece):
        where = slots.at[t, slot, pl.ds(piece * H, H), :]
        remote(where, where, rs_send.at[t, 0, piece], rs_recv.at[t, slot, piece], c, k, z).wait_recv()

    WIDE = 1792

    def relay(t, r, incoming):
        b = relay_block(r)
        for piece in range(2):
            part = pl.ds(piece * H, H)
            if incoming:
                rs_wait(t, b, piece)

            def one(i, carry):
                c0 = pl.multiple_of(i * WIDE, WIDE)
                x = acc[lax.rem(t, 3), b, part, pl.ds(c0, WIDE)]
                if incoming:
                    x = x + slots[t, b, part, pl.ds(c0, WIDE)].astype(f32)
                slots[t, b, part, pl.ds(c0, WIDE)] = x.astype(bf)
                return carry
            lax.fori_loop(0, D // WIDE, one, 0)
            rs_copy(t, b, piece).start()

    def out_copy(t, piece):
        return remote(
            stage.at[t, pl.ds(piece * H, H), :],
            out_ref.at[pl.ds(pl.multiple_of(c * B + piece * H, H), H), :],
            out_send.at[t, piece], out_recv.at[c, piece], t, k, z,
        )

    def finish(t):
        for piece in range(2):
            @pl.when(z > 0)
            def _():
                rs_wait(t, z, piece)

            @pl.when(z < n - 1)
            def _():
                rs_wait(t, n, piece)

            part = pl.ds(piece * H, H)
            x = acc[lax.rem(t, 3), z, part, :]
            x = x + jnp.where(z > 0, slots[t, z, part, :].astype(f32), 0.0)
            x = x + jnp.where(z < n - 1, slots[t, n, part, :].astype(f32), 0.0)
            y = x * lax.rsqrt(jnp.mean(x * x, axis=-1, keepdims=True) + EPSILON) * post_ref[...].reshape(1, D)
            y = (act_in[t, part, :].astype(f32) + y).astype(bf)

            @pl.when(t == c)
            def _():
                out_ref[pl.ds(pl.multiple_of(c * B + piece * H, H), H), :] = y

            @pl.when(t != c)
            def _():
                stage[t, part, :] = y

            @pl.when(t != c)
            def _():
                out_copy(t, piece).start()

    def spread():
        for d in range(3):
            spread_copy(2 - d).start()

    @pl.when(c == 0)
    def _():
        spread()

    act_in[c] = act_ref[pl.ds(pl.multiple_of(c * B, B), B), :]
    normalize(c)
    forward(c, z, True, True)

    @pl.when(c != 0)
    def _():
        spread()
        normalize(0)
        forward(0, z, True, True)

    for x in cache_copies + weight_copies:
        x.wait()

    def own_rows(t):
        @pl.when(t != c)
        def _():
            normalize(t)
            forward(t, z, True, True)

    def slot_step(t, carry):
        gathers = t < PHASES
        computes = (t >= 1) & (t <= PHASES)
        sums = (t >= 2) & inner

        @pl.when(computes)
        def _():
            project(t - 1, 1 - near)
            send_kv(t - 1, 1 - near)

        @pl.when(gathers)
        def _():
            hop(t, 1)

        @pl.when((t >= 1) & (t + 1 < PHASES) & inner)
        def _():
            own_rows(t + 1)

        @pl.when(gathers)
        def _():
            project(t, near)

        @pl.when(t >= 3)
        def _():
            finish(t - 3)

        @pl.when(sums)
        def _():
            relay(t - 2, 0, True)

        @pl.when(computes)
        def _():
            for half in range(2):
                for core in range(2):
                    for d in range(3):
                        kv_copy(t - 1, half, core, d, chip_at(d)).wait_recv()

        @pl.when(gathers)
        def _():
            send_kv(t, near)

        @pl.when(computes)
        def _():
            attend_half(t - 1, 1 - near)

            @pl.when(outer)
            def _():
                for r in range(2):
                    relay(t - 1, r, False)

        @pl.when(gathers)
        def _():
            hop(t, 2)

        @pl.when(t == 0)
        def _():
            def early(q, carry):
                @pl.when(outer | (q == 1))
                def _():
                    own_rows(q)
                return carry
            lax.fori_loop(1, PHASES, early, 0)

        @pl.when(sums)
        def _():
            relay(t - 2, 1, True)

        @pl.when(computes)
        def _():
            attend_half(t - 1, near)

            @pl.when(outer)
            def _():
                relay(t - 1, 2, False)

        @pl.when(sums)
        def _():
            relay(t - 2, 2, True)

        @pl.when(gathers)
        def _():
            hop(t, 3)
        return carry

    lax.fori_loop(0, PHASES + 2, slot_step, 0)
    finish(PHASES - 1)

    for d in range(3):
        chip = chip_at(d)
        for piece in range(2):
            where = out_ref.at[pl.ds(pl.multiple_of(chip * B + piece * H, H), H), :]
            remote(where, where, out_send.at[0, piece], out_recv.at[chip, piece], c, k, z).wait_recv()

    for d in range(3):
        spread_copy(d).wait_send()

    def drain(t, carry):
        def blocks(b, carry):
            @pl.when((b <= z) & (z < n - 1))
            def _():
                ag_copy(t, 0, b).wait_send()

            @pl.when((b >= z) & (z > 0))
            def _():
                ag_copy(t, 1, b).wait_send()

            core_copy(t, b, k).wait_send()

            @pl.when(b != z)
            def _():
                for piece in range(2):
                    rs_copy(t, b, piece).wait_send()
            return carry
        lax.fori_loop(0, n, blocks, 0)
        for half in range(2):
            for core in range(2):
                for d in range(3):
                    kv_copy(t, half, core, d, c).wait_send()
        for half in range(2):
            att_copy(t, half, k).wait_send()

        @pl.when(t != c)
        def _():
            for piece in range(2):
                out_copy(t, piece).wait_send()
        return carry
    lax.fori_loop(0, PHASES, drain, 0)


def phased_per_device(act, gain, wq, wk, wv, wo, cache, post):
    R, D = act.shape
    n = 4
    B = R // CHIPS
    c = lax.axis_index("seq") // CORES
    t, half, core, zz = jnp.meshgrid(*[jnp.arange(x, dtype=jnp.int32) for x in (PHASES, 2, 2, 2)], indexing="ij")
    starts = TOK_DEV * (2 * t + core) + R * (2 * half + zz) + B * c
    positions = jnp.concatenate([starts.reshape(-1), jnp.arange(B, dtype=jnp.int32)])
    cosine, sine = rope_tables(positions.astype(jnp.float32))
    blocks = starts.size
    far = [x[:blocks].reshape(blocks, 1, HD) for x in (cosine, sine)]
    low = [x[blocks:] for x in (cosine, sine)]
    bf, f32 = jnp.bfloat16, jnp.float32
    vmem = pl.BlockSpec(memory_space=pltpu.VMEM)
    hbm = pl.BlockSpec(memory_space=pl.ANY)
    dma = pltpu.SemaphoreType.DMA
    KW, QW = wk.shape[1] // CORES, wq.shape[1] // CORES
    cache = cache.reshape(2, 4, 2, CHIPS, B, wk.shape[1])
    return pl.pallas_call(
        phased_kernel,
        out_shape=jax.ShapeDtypeStruct((R, D), bf),
        in_specs=[vmem, vmem, hbm, hbm, hbm, hbm, hbm, vmem, vmem, vmem, vmem, vmem],
        out_specs=vmem,
        scratch_shapes=[
            pltpu.VMEM((D, 2 * KW + QW), bf),
            pltpu.VMEM(wo.shape, bf),
            pltpu.VMEM((PHASES, B, D), bf),
            pltpu.VMEM((PHASES, 2, CORES, 2, B, D), bf),
            pltpu.VMEM((PHASES, 2, CORES, 2 * B, QW), bf),
            pltpu.VMEM((4 + 4 * PHASES, 2, CHIPS, B, 2 * KW), bf),
            pltpu.VMEM((PHASES, 2, 2 * B, CORES * QW), bf),
            pltpu.VMEM((PHASES, 2, 2 * B, QW), bf),
            pltpu.VMEM((PHASES, n + 1, B, D), bf),
            pltpu.VMEM((3, n, B, D), f32),
            pltpu.VMEM((PHASES, B, D), bf),
            dma((4,)),
            dma((2,)),
            dma((3,)),
            dma((CHIPS,)),
            dma((PHASES, 2, n)),
            dma((PHASES, n)),
            dma((PHASES, n)),
            dma((PHASES, n)),
            dma((PHASES, 2, CORES, 3)),
            dma((PHASES, 2, CORES, 3)),
            dma((PHASES, 2)),
            dma((PHASES, 2)),
            dma((PHASES, n, 2)),
            dma((PHASES, n + 1, 2)),
            dma((PHASES, 2)),
            dma((CHIPS, 2)),
        ],
        compiler_params=pltpu.CompilerParams(
            collective_id=1, has_side_effects=True, vmem_limit_bytes=62 * 1024 * 1024
        ),
    )(act, gain, wq, wk, wv, wo, cache, post, *far, *low)


def solution(mesh):
    if mesh.shape["head"] == 4 and mesh.shape["seq"] == CHIPS * CORES:
        body = phased_per_device
    else:
        body = functools.partial(per_device, mesh.shape["head"], mesh.shape["seq"])
    return jax.shard_map(
        body,
        mesh=mesh,
        in_specs=(
            P(("seq", "head"), None),
            P(),
            P(None, "head"),
            P(None, "head"),
            P(None, "head"),
            P("head", None),
            P(None, None, "head"),
            P(),
        ),
        out_specs=P(("seq", "head"), None),
        check_vma=False,
    )
```

```python
import functools
import jax
import jax.numpy as jnp
from jax import lax
from jax.experimental import pallas as pl
from jax.experimental.pallas import tpu as pltpu
from jax.sharding import PartitionSpec as P

HD = 128
WINDOW = 1024
SCALAR = 168
TOK_DEV = 512
EPSILON = 1e-06
ROPE_BASE = 10000.0
REACH = WINDOW // TOK_DEV
COL_CHUNKS = 7
MESH = pl.DeviceIdType.MESH


def rope_tables(positions):
    half_size = HD // 2
    frequency = ROPE_BASE ** (-(jnp.arange(half_size, dtype=jnp.float32) * 2.0 / HD))
    angles = positions[:, None] * frequency[None, :]
    cosine = jnp.cos(angles)
    sine = jnp.sin(angles)
    return jnp.concatenate([cosine, cosine], axis=1), jnp.concatenate([-sine, sine], axis=1)


def kernel(
    n, s_count,
    act_ref, gain_ref, wq_hbm, wk_hbm, wv_hbm, wo_hbm, cache_hbm, post_ref, cos_ref, sin_ref,
    out_ref,
    wq, wk, wv, wo, rows, q_buf, kv, att, slots, acc,
    w_sem, cache_sem, ag_send, ag_recv, kv_send, kv_recv, rs_send, rs_recv,
):
    s = lax.axis_index("seq")
    z = lax.axis_index("head")
    R, D = act_ref.shape
    kv_width = wk.shape[1]
    heads_kv = kv_width // HD
    group = wq.shape[1] // kv_width
    row_chunks = ag_send.shape[2]
    CR = R // row_chunks
    CD = D // COL_CHUNKS

    weight_copies = [
        pltpu.make_async_copy(src, dst, w_sem.at[i])
        for i, (src, dst) in enumerate([(wk_hbm, wk), (wv_hbm, wv), (wq_hbm, wq), (wo_hbm, wo)])
    ]
    for c in weight_copies:
        c.start()

    def cache_copies(d):
        return [
            pltpu.make_async_copy(
                cache_hbm.at[i, pl.ds(pl.multiple_of(WINDOW + (s - d) * TOK_DEV, TOK_DEV), TOK_DEV), :],
                kv.at[pl.ds(WINDOW - d * TOK_DEV, TOK_DEV), pl.ds(i * kv_width, kv_width)],
                cache_sem.at[d - 1, i],
            )
            for i in range(2)
        ]

    for d in range(1, REACH + 1):
        @pl.when(s < d)
        def _():
            for c in cache_copies(d):
                c.start()

    barrier = pltpu.get_barrier_semaphore()

    def greet(cond, ds, dz):
        @pl.when(cond)
        def _():
            pl.semaphore_signal(barrier, inc=1, device_id=(s + ds, z + dz), device_id_type=MESH)

    partners = [(z > 0, 0, -1), (z < n - 1, 0, 1)]
    for d in range(1, REACH + 1):
        partners += [(s >= d, -d, 0), (s + d < s_count, d, 0)]
    for p in partners:
        greet(*p)

    def norm_chunk(i, carry):
        r0 = pl.multiple_of(i * 16, 16)
        x = act_ref[pl.ds(r0, 16), :].astype(jnp.float32)
        y = x * lax.rsqrt(jnp.mean(x * x, axis=-1, keepdims=True) + EPSILON) * gain_ref[...].reshape(1, D)
        rows[z, pl.ds(r0, 16), :] = y.astype(jnp.bfloat16)
        return carry

    pl.semaphore_wait(barrier, sum(jnp.where(p[0], 1, 0) for p in partners))

    right = lax.rem(z + 1, n)
    left = lax.rem(z + n - 1, n)

    def ag_copy(direction, block, c):
        where = rows.at[block, pl.ds(c * CR, CR), :]
        return pltpu.make_async_remote_copy(
            src_ref=where, dst_ref=where,
            send_sem=ag_send.at[direction, block, c], recv_sem=ag_recv.at[direction, block, c],
            device_id=(s, right if direction == 0 else left), device_id_type=MESH,
        )

    def kv_copy(d, block):
        r0 = pl.multiple_of(block * R, R)
        return pltpu.make_async_remote_copy(
            src_ref=kv.at[pl.ds(WINDOW + r0, R), :],
            dst_ref=kv.at[pl.ds(WINDOW - d * TOK_DEV + r0, R), :],
            send_sem=kv_send.at[d - 1, block], recv_sem=kv_recv.at[d - 1, block],
            device_id=(lax.rem(s + d, s_count), z), device_id_type=MESH,
        )

    def rs_copy(direction, block, slot, c):
        where = slots.at[slot, c]
        return pltpu.make_async_remote_copy(
            src_ref=where, dst_ref=where,
            send_sem=rs_send.at[direction, block, c], recv_sem=rs_recv.at[direction, block, c],
            device_id=(s, right if direction == 0 else left), device_id_type=MESH,
        )

    def project(block):
        r0 = pl.multiple_of(block * R, R)
        cosine = cos_ref[pl.ds(r0, R), :]
        sine = sin_ref[pl.ds(r0, R), :]

        def run(w, tile, rotary, scale, dst, dst_r0, dst_c0):
            def one(i, carry):
                c0 = pl.multiple_of(i * tile, tile)
                t = jnp.dot(rows[block], w[:, pl.ds(c0, tile)], preferred_element_type=jnp.float32)
                for h in range(tile // HD):
                    u = t[:, h * HD:(h + 1) * HD]
                    if rotary:
                        u = u * cosine + pltpu.roll(u, HD // 2, 1) * sine
                    if scale is not None:
                        u = u * scale
                    dst[pl.ds(dst_r0, R), pl.ds(pl.multiple_of(dst_c0 + c0 + h * HD, HD), HD)] = u.astype(jnp.bfloat16)
                return carry
            lax.fori_loop(0, w.shape[1] // tile, one, 0)

        tile = min(256, kv_width)
        own = pl.multiple_of(WINDOW + r0, R)
        run(wk, tile, True, None, kv, own, 0)
        run(wv, tile, False, None, kv, own, kv_width)
        for d in range(1, REACH + 1):
            @pl.when(s + d < s_count)
            def _():
                kv_copy(d, block).start()
        run(wq, 256, True, SCALAR ** (-0.5), q_buf, r0, 0)

    for c in range(row_chunks):
        lax.fori_loop(c * CR // 16, (c + 1) * CR // 16, norm_chunk, 0)

        @pl.when(z < n - 1)
        def _():
            ag_copy(0, z, c).start()

        @pl.when(z > 0)
        def _():
            ag_copy(1, z, c).start()

    for i in range(3):
        weight_copies[i].wait()
    def gather_step(t, carry):
        from_left = z - t
        from_right = z + t
        for c in range(row_chunks):
            @pl.when(from_left >= 0)
            def _():
                ag_copy(0, from_left, c).wait_recv()

                @pl.when(z < n - 1)
                def _():
                    ag_copy(0, from_left, c).start()

            @pl.when(from_right < n)
            def _():
                ag_copy(1, from_right, c).wait_recv()

                @pl.when(z > 0)
                def _():
                    ag_copy(1, from_right, c).start()

            if c == 0:
                @pl.when(from_right - 1 < n)
                def _():
                    project(from_right - 1)

        @pl.when(from_left >= 0)
        def _():
            project(from_left)
        return carry

    lax.fori_loop(1, n, gather_step, 0)

    @pl.when(z == 0)
    def _():
        project(n - 1)

    for d in range(1, REACH + 1):
        @pl.when(s < d)
        def _():
            for c in cache_copies(d):
                c.wait()

        @pl.when(s >= d)
        def _():
            lax.fori_loop(0, n, lambda b, carry: (kv_copy(d, b).wait_recv(), carry)[1], 0)
    weight_copies[3].wait()

    row_i = lax.broadcasted_iota(jnp.int32, (group * R, R), 0)
    row_i = lax.rem(row_i, R)
    col_i = lax.broadcasted_iota(jnp.int32, (group * R, R), 1)
    later = col_i > row_i
    spans = [(0, R), (R, WINDOW - R), (WINDOW, R)]

    def attend(block):
        r0 = pl.multiple_of(block * R, R)
        for g in range(heads_kv):
            q = jnp.concatenate(
                [q_buf[pl.ds(r0, R), (g * group + a) * HD:(g * group + a + 1) * HD] for a in range(group)], axis=0
            )
            scores = []
            for j, (o, w) in enumerate(spans):
                k = kv[pl.ds(pl.multiple_of(r0 + o, R), w), g * HD:(g + 1) * HD]
                sc = lax.dot_general(q, k, (((1,), (1,)), ((), ())), preferred_element_type=jnp.float32)
                if j == 0:
                    sc = jnp.where(later, sc, -jnp.inf)
                if j == 2:
                    sc = jnp.where(later, -jnp.inf, sc)
                scores.append(sc)
            m = functools.reduce(jnp.maximum, [jnp.max(x, axis=-1, keepdims=True) for x in scores])
            total = 0.0
            o_sum = 0.0
            for (o, w), sc in zip(spans, scores):
                e = jnp.exp(sc - m)
                total = total + jnp.sum(e, axis=-1, keepdims=True)
                v = kv[pl.ds(pl.multiple_of(r0 + o, R), w), kv_width + g * HD:kv_width + (g + 1) * HD]
                o_sum = o_sum + jnp.dot(e.astype(jnp.bfloat16), v, preferred_element_type=jnp.float32)
            o_sum = (o_sum / total).astype(jnp.bfloat16)
            for a in range(group):
                att[:, (g * group + a) * HD:(g * group + a + 1) * HD] = o_sum[a * R:(a + 1) * R]

    TILE = 256

    def partial_out(direction, block, incoming):
        attend(block)
        for c in range(COL_CHUNKS):
            @pl.when(incoming)
            def _():
                rs_copy(direction, block, block, c).wait_recv()

            def one(i, carry):
                c0 = pl.multiple_of(i * TILE, TILE)
                w0 = pl.multiple_of(c * CD + i * TILE, TILE)
                p = jnp.dot(att[...], wo[:, pl.ds(w0, TILE)], preferred_element_type=jnp.float32)
                before = slots[block, c, :, pl.ds(c0, TILE)].astype(jnp.float32)
                p = p + jnp.where(incoming, before, 0.0)
                slots[block, c, :, pl.ds(c0, TILE)] = p.astype(jnp.bfloat16)
                return carry
            lax.fori_loop(0, CD // TILE, one, 0)
            send_out(direction, block, c).start()

    def send_out(direction, block, c):
        if direction == 0:
            return rs_copy(0, block, block, c)
        last = jnp.where(block == z - 1, n, block)
        return pltpu.make_async_remote_copy(
            src_ref=slots.at[block, c], dst_ref=slots.at[last, c],
            send_sem=rs_send.at[1, block, c], recv_sem=rs_recv.at[1, block, c],
            device_id=(s, left), device_id_type=MESH,
        )

    def scatter_step(t, carry):
        to_right = n - t
        to_left = t - 1

        @pl.when(to_right > z)
        def _():
            partial_out(0, to_right, z > 0)

        @pl.when(to_left < z)
        def _():
            partial_out(1, to_left, z < n - 1)
        return carry

    lax.fori_loop(1, n, scatter_step, 0)

    attend(z)

    def own(i, carry):
        w0 = pl.multiple_of(i * TILE, TILE)
        acc[:, pl.ds(w0, TILE)] = jnp.dot(att[...], wo[:, pl.ds(w0, TILE)], preferred_element_type=jnp.float32)
        return carry
    lax.fori_loop(0, D // TILE, own, 0)

    for c in range(COL_CHUNKS):
        for direction, slot, cond in ((0, z, z > 0), (1, n, z < n - 1)):
            @pl.when(cond)
            def _():
                rs_copy(direction, z, slot, c).wait_recv()
                acc[:, c * CD:(c + 1) * CD] += slots[slot, c].astype(jnp.float32)

    def finish(i, carry):
        r0 = pl.multiple_of(i * 16, 16)
        x = acc[pl.ds(r0, 16), :]
        y = x * lax.rsqrt(jnp.mean(x * x, axis=-1, keepdims=True) + EPSILON) * post_ref[...].reshape(1, D)
        out_ref[pl.ds(r0, 16), :] = (act_ref[pl.ds(r0, 16), :].astype(jnp.float32) + y).astype(jnp.bfloat16)
        return carry
    lax.fori_loop(0, R // 16, finish, 0)

    def drain(b, carry):
        @pl.when((b <= z) & (z < n - 1))
        def _():
            for c in range(row_chunks):
                ag_copy(0, b, c).wait_send()

        @pl.when((b >= z) & (z > 0))
        def _():
            for c in range(row_chunks):
                ag_copy(1, b, c).wait_send()

        @pl.when(b > z)
        def _():
            for c in range(COL_CHUNKS):
                send_out(0, b, c).wait_send()

        @pl.when(b < z)
        def _():
            for c in range(COL_CHUNKS):
                send_out(1, b, c).wait_send()

        for d in range(1, REACH + 1):
            @pl.when(s + d < s_count)
            def _():
                kv_copy(d, b).wait_send()
        return carry
    lax.fori_loop(0, n, drain, 0)


def per_device(n, s_count, act, gain, wq, wk, wv, wo, cache, post):
    R, D = act.shape
    row_chunks = min(4, R // 16)
    s = lax.axis_index("seq")
    positions = (s * TOK_DEV + jnp.arange(TOK_DEV, dtype=jnp.int32)).astype(jnp.float32)
    cosine, sine = rope_tables(positions)
    bf, f32 = jnp.bfloat16, jnp.float32
    vmem = pl.BlockSpec(memory_space=pltpu.VMEM)
    hbm = pl.BlockSpec(memory_space=pl.ANY)
    dma = pltpu.SemaphoreType.DMA
    return pl.pallas_call(
        functools.partial(kernel, n, s_count),
        out_shape=jax.ShapeDtypeStruct((R, D), bf),
        in_specs=[vmem, vmem, hbm, hbm, hbm, hbm, hbm, vmem, vmem, vmem],
        out_specs=vmem,
        scratch_shapes=[
            pltpu.VMEM(wq.shape, bf),
            pltpu.VMEM(wk.shape, bf),
            pltpu.VMEM(wv.shape, bf),
            pltpu.VMEM(wo.shape, bf),
            pltpu.VMEM((n, R, D), bf),
            pltpu.VMEM((TOK_DEV, wq.shape[1]), bf),
            pltpu.VMEM((WINDOW + TOK_DEV, 2 * wk.shape[1]), bf),
            pltpu.VMEM((R, wo.shape[0]), bf),
            pltpu.VMEM((n + 1, COL_CHUNKS, R, D // COL_CHUNKS), bf),
            pltpu.VMEM((R, D), f32),
            dma((4,)),
            dma((REACH, 2)),
            dma((2, n, row_chunks)),
            dma((2, n, row_chunks)),
            dma((REACH, n)),
            dma((REACH, n)),
            dma((2, n, COL_CHUNKS)),
            dma((2, n, COL_CHUNKS)),
        ],
        compiler_params=pltpu.CompilerParams(
            collective_id=0, has_side_effects=True, vmem_limit_bytes=62 * 1024 * 1024
        ),
    )(act, gain, wq, wk, wv, wo, cache, post, cosine, sine)


PHASES = 4
CHIPS = 4
CORES = 2


def phased_kernel(
    act_ref, gain_ref, wq_hbm, wk_hbm, wv_hbm, wo_hbm, cache_hbm, post_ref, far_cos, far_sin, low_cos, low_sin,
    out_ref,
    w, wo, act_in, rows, q_buf, kv, att, att_x, slots, acc, stage,
    w_sem, cache_sem, spread_send, spread_recv, ag_send, ag_recv, core_send, core_recv,
    kv_send, kv_recv, att_send, att_recv, rs_send, rs_recv, out_send, out_recv, go_sem,
):
    n = 4
    s = lax.axis_index("seq")
    z = lax.axis_index("head")
    c = s // CORES
    k = lax.rem(s, CORES)
    B, D = act_in.shape[1:]
    KW = wk_hbm.shape[1] // CORES
    QW = wq_hbm.shape[1] // CORES
    heads_kv = KW // HD
    group = QW // KW
    bf, f32 = jnp.bfloat16, jnp.float32
    near = z // 2
    inner = (z > 0) & (z < n - 1)
    outer = (z == 0) | (z == n - 1)

    def remote(src, dst, send, recv, chip, core, plane):
        return pltpu.make_async_remote_copy(
            src_ref=src, dst_ref=dst, send_sem=send, recv_sem=recv,
            device_id=(chip * CORES + core, plane), device_id_type=MESH,
        )

    def chip_at(d):
        return [c + 1 - 2 * lax.rem(c, 2), lax.rem(c + 2, CHIPS), CHIPS - 1 - c][d]

    weight_copies = [
        pltpu.make_async_copy(wk_hbm.at[:, pl.ds(pl.multiple_of(k * KW, KW), KW)], w.at[:, pl.ds(0, KW)], w_sem.at[0]),
        pltpu.make_async_copy(wv_hbm.at[:, pl.ds(pl.multiple_of(k * KW, KW), KW)], w.at[:, pl.ds(KW, KW)], w_sem.at[1]),
        pltpu.make_async_copy(wq_hbm.at[:, pl.ds(pl.multiple_of(k * QW, QW), QW)], w.at[:, pl.ds(2 * KW, QW)], w_sem.at[2]),
        pltpu.make_async_copy(wo_hbm, wo, w_sem.at[3]),
    ]
    cache_copies = [
        pltpu.make_async_copy(
            cache_hbm.at[i, :, :, :, :, pl.ds(pl.multiple_of(k * KW, KW), KW)],
            kv.at[pl.ds(0, 4), :, :, :, pl.ds(i * KW, KW)],
            cache_sem.at[i],
        )
        for i in range(2)
    ]

    barrier = pltpu.get_barrier_semaphore()

    def greet(chip, core, plane):
        pl.semaphore_signal(barrier, inc=1, device_id=(chip * CORES + core, plane), device_id_type=MESH)

    for d in range(3):
        greet(chip_at(d), k, z)
    greet(c, 1 - k, z)

    @pl.when(z > 0)
    def _():
        greet(c, k, z - 1)

    @pl.when(z < n - 1)
    def _():
        greet(c, k, z + 1)

    for x in weight_copies + cache_copies:
        x.start()
    pl.semaphore_wait(barrier, 4 + jnp.where(inner, 2, 1))

    def spread_copy(d):
        to = chip_at(d)
        return remote(
            act_ref.at[pl.ds(pl.multiple_of(to * B, B), B), :], act_in.at[c],
            spread_send.at[d], spread_recv.at[c], to, k, z,
        )

    def spread_wait(t):
        remote(act_in.at[t], act_in.at[t], spread_send.at[0], spread_recv.at[t], c, k, z).wait_recv()

    def ag_copy(t, direction, zb):
        where = rows.at[2 * t + k, zb]
        to = jnp.minimum(z + 1, n - 1) if direction == 0 else jnp.maximum(z - 1, 0)
        return remote(where, where, ag_send.at[t, direction, zb], ag_recv.at[t, zb], c, k, to)

    def core_copy(u, zb):
        where = rows.at[u, zb]
        return remote(where, where, core_send.at[u // 2, zb], core_recv.at[u // 2, zb], c, 1 - k, z)

    def normalize(t):
        @pl.when(t != c)
        def _():
            spread_wait(t)

        def piece(i, carry):
            r0 = pl.multiple_of(i * 16, 16)
            x = act_in[t, pl.ds(r0, 16), :].astype(f32)
            y = x * lax.rsqrt(jnp.mean(x * x, axis=-1, keepdims=True) + EPSILON) * gain_ref[...].reshape(1, D)
            rows[2 * t + k, z, pl.ds(r0, 16), :] = y.astype(bf)
            return carry
        lax.fori_loop(0, B // 16, piece, 0)

    def forward(t, zb, right, left):
        if right:
            @pl.when(z < n - 1)
            def _():
                ag_copy(t, 0, zb).start()
        if left:
            @pl.when(z > 0)
            def _():
                ag_copy(t, 1, zb).start()
        core_copy(2 * t + k, zb).start()

    def hop(t, h):
        @pl.when(z - h >= 0)
        def _():
            ag_copy(t, 0, z - h).wait_recv()
            forward(t, z - h, True, False)

        @pl.when(z + h < n)
        def _():
            ag_copy(t, 1, z + h).wait_recv()
            forward(t, z + h, False, True)

    def kv_copy(u, d, chip):
        where = kv.at[pl.ds(4 + 2 * u, 2), :, chip]
        return remote(where, where, kv_send.at[u, d], kv_recv.at[u, d], chip_at(d), k, z)

    def project(u):
        @pl.when(lax.rem(u, 2) != k)
        def _():
            for zb in range(n):
                core_copy(u, zb).wait_recv()

        cosine, sine = [], []
        for i in range(n):
            ca, sa = far_cos[4 * u + i], far_sin[4 * u + i]
            cb, sb = low_cos[...], low_sin[...]
            cosine.append(ca * cb - sa * sb)
            sine.append(sa * cb + ca * sb)
        cosine = jnp.concatenate(cosine, axis=0)
        sine = jnp.concatenate(sine, axis=0)

        def matmul(c0, width):
            return jnp.dot(
                rows[u].reshape(n * B, D), w[:, pl.ds(c0, width)], preferred_element_type=f32
            )

        def rope(x):
            return x * cosine + pltpu.roll(x, HD // 2, 1) * sine

        for part in range(2):
            x = matmul(part * KW, KW)
            for h in range(heads_kv):
                v = x[:, h * HD:(h + 1) * HD]
                v = (rope(v) if part == 0 else v).astype(bf)
                c0 = part * KW + h * HD
                for zb in range(n):
                    kv[4 + 2 * u + zb // 2, zb % 2, c, :, c0:c0 + HD] = v[zb * B:(zb + 1) * B]
        for d in range(3):
            kv_copy(u, 2 - d, c).start()

        def queries(i, carry):
            c0 = pl.multiple_of(i * 256, 256)
            x = matmul(2 * KW + c0, 256)
            for h in range(256 // HD):
                v = (rope(x[:, h * HD:(h + 1) * HD]) * SCALAR ** (-0.5)).astype(bf)
                for half in range(2):
                    q_buf[u, half, :, pl.ds(pl.multiple_of(c0 + h * HD, HD), HD)] = v[half * 2 * B:(half + 1) * 2 * B]
            return carry
        lax.fori_loop(0, QW // 256, queries, 0)

    M = group * 2 * B
    row = lax.rem(lax.broadcasted_iota(jnp.int32, (M, 256), 0), 2 * B)
    place = (row // B) * (CHIPS * B) + lax.rem(row, B) + c * B
    later = lax.broadcasted_iota(jnp.int32, (M, 256), 1) > place
    spans = [(0, 1), (1, 3), (4, 1)]

    def attend(unit, half, dst, dst_c0):
        t = unit // 2
        u = 2 * unit + half
        for g in range(heads_kv):
            q = jnp.concatenate(
                [q_buf[unit, half, :, (g * group + a) * HD:(g * group + a + 1) * HD] for a in range(group)], axis=0
            )
            scores = []
            for j, (o, wd) in enumerate(spans):
                key = kv[pl.ds(u + o, wd), :, :, :, g * HD:(g + 1) * HD].reshape(wd * 256, HD)
                sc = lax.dot_general(q, key, (((1,), (1,)), ((), ())), preferred_element_type=f32)
                if j == 0:
                    sc = jnp.where(later, sc, -jnp.inf)
                if j == 2:
                    sc = jnp.where(later, -jnp.inf, sc)
                scores.append(sc)
            m = functools.reduce(jnp.maximum, [jnp.max(x, axis=-1, keepdims=True) for x in scores])
            total = 0.0
            o_sum = 0.0
            for (o, wd), sc in zip(spans, scores):
                e = jnp.exp(sc - m)
                total = total + jnp.sum(e, axis=-1, keepdims=True)
                v = kv[pl.ds(u + o, wd), :, :, :, KW + g * HD:KW + (g + 1) * HD].reshape(wd * 256, HD)
                o_sum = o_sum + jnp.dot(e.astype(bf), v, preferred_element_type=f32)
            o_sum = (o_sum / total).astype(bf)
            for a in range(group):
                c0 = dst_c0 + (g * group + a) * HD
                dst[t, half, :, pl.ds(pl.multiple_of(c0, HD), HD)] = o_sum[a * 2 * B:(a + 1) * 2 * B]

    def attend_halves(u, dst, dst_c0):
        def one(half, carry):
            attend(u, half, dst, dst_c0)
            return carry
        lax.fori_loop(0, 2, one, 0)

    def att_copy(t, core):
        return remote(
            att_x.at[t], att.at[t, :, :, pl.ds(pl.multiple_of(core * QW, QW), QW)],
            att_send.at[t], att_recv.at[t], c, 1 - k, z,
        )

    TILE = 1792

    def project_out(t):
        def one(i, carry):
            w0 = pl.multiple_of(i * TILE, TILE)
            p = jnp.dot(att[t].reshape(n * B, CORES * QW), wo[:, pl.ds(w0, TILE)], preferred_element_type=f32)
            acc[lax.rem(t, 2), :, :, pl.ds(w0, TILE)] = p.reshape(n, B, TILE)
            return carry
        lax.fori_loop(0, D // TILE, one, 0)

    def relay_block(r):
        low = z < 2
        if r == 0:
            return jnp.where(low, n - 1, 0)
        if r == 1:
            return jnp.where(low, n - 2, 1)
        return z + 1 - 2 * lax.rem(z, 2)

    H = B // 2

    def rs_copy(t, b, piece):
        to = jnp.where(b > z, z + 1, z - 1)
        slot = jnp.where(b == z - 1, n, b)
        part = pl.ds(piece * H, H)
        return remote(
            slots.at[t, b, part, :], slots.at[t, slot, part, :],
            rs_send.at[t, b, piece], rs_recv.at[t, slot, piece], c, k, to,
        )

    def rs_wait(t, slot, piece):
        where = slots.at[t, slot, pl.ds(piece * H, H), :]
        remote(where, where, rs_send.at[t, 0, piece], rs_recv.at[t, slot, piece], c, k, z).wait_recv()

    WIDE = 1792

    def relay(t, r, incoming):
        b = relay_block(r)
        for piece in range(2):
            part = pl.ds(piece * H, H)
            if incoming:
                rs_wait(t, b, piece)

            def one(i, carry):
                c0 = pl.multiple_of(i * WIDE, WIDE)
                x = acc[lax.rem(t, 2), b, part, pl.ds(c0, WIDE)]
                if incoming:
                    x = x + slots[t, b, part, pl.ds(c0, WIDE)].astype(f32)
                slots[t, b, part, pl.ds(c0, WIDE)] = x.astype(bf)
                return carry
            lax.fori_loop(0, D // WIDE, one, 0)
            rs_copy(t, b, piece).start()

    def out_copy(t, piece):
        return remote(
            stage.at[t, pl.ds(piece * H, H), :],
            out_ref.at[pl.ds(pl.multiple_of(c * B + piece * H, H), H), :],
            out_send.at[t, piece], out_recv.at[c, piece], t, k, z,
        )

    def finish(t):
        for piece in range(2):
            @pl.when(z > 0)
            def _():
                rs_wait(t, z, piece)

            @pl.when(z < n - 1)
            def _():
                rs_wait(t, n, piece)

            part = pl.ds(piece * H, H)
            x = acc[lax.rem(t, 2), z, part, :]
            x = x + jnp.where(z > 0, slots[t, z, part, :].astype(f32), 0.0)
            x = x + jnp.where(z < n - 1, slots[t, n, part, :].astype(f32), 0.0)
            y = x * lax.rsqrt(jnp.mean(x * x, axis=-1, keepdims=True) + EPSILON) * post_ref[...].reshape(1, D)
            y = (act_in[t, part, :].astype(f32) + y).astype(bf)

            @pl.when(t == c)
            def _():
                out_ref[pl.ds(pl.multiple_of(c * B + piece * H, H), H), :] = y

            @pl.when(t != c)
            def _():
                stage[t, part, :] = y

            @pl.when(t != c)
            def _():
                out_copy(t, piece).start()

    def spread():
        for d in range(3):
            spread_copy(2 - d).start()

    @pl.when((c == 0) & (k == 0))
    def _():
        spread()

    act_in[c] = act_ref[pl.ds(pl.multiple_of(c * B, B), B), :]
    normalize(c)
    forward(c, z, True, True)

    @pl.when((c == 0) & (k == 0))
    def _():
        for d in range(3):
            spread_copy(d).wait_send()
        pl.semaphore_signal(go_sem, inc=1, device_id=(s + 1, z), device_id_type=MESH)

    @pl.when((c == 0) & (k == 1))
    def _():
        pl.semaphore_wait(go_sem, 1)
        spread()

    @pl.when(c != 0)
    def _():
        @pl.when(k == 0)
        def _():
            normalize(0)
            forward(0, z, True, True)
        spread()

    for x in cache_copies + weight_copies:
        x.wait()

    UNITS = PHASES * CORES

    def own_rows(t):
        @pl.when((t != c) & (t + k > 0))
        def _():
            normalize(t)
            forward(t, z, True, True)

    def step(j, carry):
        mine = lax.rem(j, 2) == k
        gathers = mine & (j < UNITS)
        attends = (j >= 2) & (j <= UNITS + 1)
        sums = (~mine) & inner & (j >= 3)
        t = j // 2
        behind = (j - 3) // 2

        @pl.when(gathers)
        def _():
            hop(t, 1)

        @pl.when((~mine) & (j + 1 < UNITS) & (inner | (j == 0)))
        def _():
            own_rows((j + 1) // 2)

        @pl.when((j >= 1) & (j <= UNITS))
        def _():
            project(j - 1)

        @pl.when(attends)
        def _():
            for d in range(3):
                kv_copy(j - 2, d, chip_at(d)).wait_recv()

            @pl.when(~mine)
            def _():
                attend_halves(j - 2, att_x, 0)
                att_copy(t - 1, k).start()

            @pl.when(mine)
            def _():
                attend_halves(j - 2, att, k * QW)
                att_copy(t - 1, 1 - k).wait_recv()
                project_out(t - 1)

                @pl.when(outer)
                def _():
                    for r in range(3):
                        relay(t - 1, r, False)

        @pl.when(sums)
        def _():
            relay(behind, 0, True)

        @pl.when(gathers)
        def _():
            hop(t, 2)

        @pl.when(outer & mine & (j <= 1))
        def _():
            lax.fori_loop(1, PHASES, lambda q, carry: (own_rows(q), carry)[1], 0)

        @pl.when(sums)
        def _():
            relay(behind, 1, True)

        @pl.when(mine & (j >= 4))
        def _():
            finish(t - 2)

        @pl.when(gathers)
        def _():
            hop(t, 3)

        @pl.when(sums)
        def _():
            relay(behind, 2, True)
        return carry

    lax.fori_loop(0, UNITS + 3, step, 0)

    @pl.when(k == 1)
    def _():
        finish(PHASES - 1)

    for d in range(3):
        chip = chip_at(d)
        for piece in range(2):
            where = out_ref.at[pl.ds(pl.multiple_of(chip * B + piece * H, H), H), :]
            remote(where, where, out_send.at[0, piece], out_recv.at[chip, piece], c, k, z).wait_recv()

    @pl.when((c > 0) | (k > 0))
    def _():
        for d in range(3):
            spread_copy(d).wait_send()

    def drain(t, carry):
        def blocks(b, carry):
            @pl.when((b <= z) & (z < n - 1))
            def _():
                ag_copy(t, 0, b).wait_send()

            @pl.when((b >= z) & (z > 0))
            def _():
                ag_copy(t, 1, b).wait_send()

            core_copy(2 * t + k, b).wait_send()

            @pl.when(b != z)
            def _():
                for piece in range(2):
                    rs_copy(t, b, piece).wait_send()
            return carry
        lax.fori_loop(0, n, blocks, 0)
        for core in range(2):
            for d in range(3):
                kv_copy(2 * t + core, d, c).wait_send()
        att_copy(t, k).wait_send()

        @pl.when(t != c)
        def _():
            for piece in range(2):
                out_copy(t, piece).wait_send()
        return carry
    lax.fori_loop(0, PHASES, drain, 0)


def phased_per_device(act, gain, wq, wk, wv, wo, cache, post):
    R, D = act.shape
    n = 4
    B = R // CHIPS
    c = lax.axis_index("seq") // CORES
    starts = R * jnp.arange(PHASES * CORES * n, dtype=jnp.int32) + B * c
    positions = jnp.concatenate([starts.reshape(-1), jnp.arange(B, dtype=jnp.int32)])
    cosine, sine = rope_tables(positions.astype(jnp.float32))
    blocks = starts.size
    far = [x[:blocks].reshape(blocks, 1, HD) for x in (cosine, sine)]
    low = [x[blocks:] for x in (cosine, sine)]
    bf, f32 = jnp.bfloat16, jnp.float32
    vmem = pl.BlockSpec(memory_space=pltpu.VMEM)
    hbm = pl.BlockSpec(memory_space=pl.ANY)
    dma = pltpu.SemaphoreType.DMA
    KW, QW = wk.shape[1] // CORES, wq.shape[1] // CORES
    cache = cache.reshape(2, 4, 2, CHIPS, B, wk.shape[1])
    return pl.pallas_call(
        phased_kernel,
        out_shape=jax.ShapeDtypeStruct((R, D), bf),
        in_specs=[vmem, vmem, hbm, hbm, hbm, hbm, hbm, vmem, vmem, vmem, vmem, vmem],
        out_specs=vmem,
        scratch_shapes=[
            pltpu.VMEM((D, 2 * KW + QW), bf),
            pltpu.VMEM(wo.shape, bf),
            pltpu.VMEM((PHASES, B, D), bf),
            pltpu.VMEM((PHASES * CORES, n, B, D), bf),
            pltpu.VMEM((PHASES * CORES, 2, 2 * B, QW), bf),
            pltpu.VMEM((4 + 4 * PHASES, 2, CHIPS, B, 2 * KW), bf),
            pltpu.VMEM((PHASES, 2, 2 * B, CORES * QW), bf),
            pltpu.VMEM((PHASES, 2, 2 * B, QW), bf),
            pltpu.VMEM((PHASES, n + 1, B, D), bf),
            pltpu.VMEM((2, n, B, D), f32),
            pltpu.VMEM((PHASES, B, D), bf),
            dma((4,)),
            dma((2,)),
            dma((3,)),
            dma((CHIPS,)),
            dma((PHASES, 2, n)),
            dma((PHASES, n)),
            dma((PHASES, n)),
            dma((PHASES, n)),
            dma((PHASES * CORES, 3)),
            dma((PHASES * CORES, 3)),
            dma((PHASES,)),
            dma((PHASES,)),
            dma((PHASES, n, 2)),
            dma((PHASES, n + 1, 2)),
            dma((PHASES, 2)),
            dma((CHIPS, 2)),
            pltpu.SemaphoreType.REGULAR,
        ],
        compiler_params=pltpu.CompilerParams(
            collective_id=1, has_side_effects=True, vmem_limit_bytes=62 * 1024 * 1024
        ),
    )(act, gain, wq, wk, wv, wo, cache, post, *far, *low)


def solution(mesh):
    if mesh.shape["head"] == 4 and mesh.shape["seq"] == CHIPS * CORES:
        body = phased_per_device
    else:
        body = functools.partial(per_device, mesh.shape["head"], mesh.shape["seq"])
    return jax.shard_map(
        body,
        mesh=mesh,
        in_specs=(
            P(("seq", "head"), None),
            P(),
            P(None, "head"),
            P(None, "head"),
            P(None, "head"),
            P("head", None),
            P(None, None, "head"),
            P(),
        ),
        out_specs=P(("seq", "head"), None),
        check_vma=False,
    )
```

```python
import functools
import jax
import jax.numpy as jnp
from jax import lax
from jax.experimental import pallas as pl
from jax.experimental.pallas import tpu as pltpu
from jax.sharding import PartitionSpec as P

HD = 128
WINDOW = 1024
SCALAR = 168
TOK_DEV = 512
EPSILON = 1e-06
ROPE_BASE = 10000.0
REACH = WINDOW // TOK_DEV
COL_CHUNKS = 7
MESH = pl.DeviceIdType.MESH


def rope_tables(positions):
    half_size = HD // 2
    frequency = ROPE_BASE ** (-(jnp.arange(half_size, dtype=jnp.float32) * 2.0 / HD))
    angles = positions[:, None] * frequency[None, :]
    cosine = jnp.cos(angles)
    sine = jnp.sin(angles)
    return jnp.concatenate([cosine, cosine], axis=1), jnp.concatenate([-sine, sine], axis=1)


def kernel(
    n, s_count,
    act_ref, gain_ref, wq_hbm, wk_hbm, wv_hbm, wo_hbm, cache_hbm, post_ref, cos_ref, sin_ref,
    out_ref,
    wq, wk, wv, wo, rows, q_buf, kv, att, slots, acc,
    w_sem, cache_sem, ag_send, ag_recv, kv_send, kv_recv, rs_send, rs_recv,
):
    s = lax.axis_index("seq")
    z = lax.axis_index("head")
    R, D = act_ref.shape
    kv_width = wk.shape[1]
    heads_kv = kv_width // HD
    group = wq.shape[1] // kv_width
    row_chunks = ag_send.shape[2]
    CR = R // row_chunks
    CD = D // COL_CHUNKS

    weight_copies = [
        pltpu.make_async_copy(src, dst, w_sem.at[i])
        for i, (src, dst) in enumerate([(wk_hbm, wk), (wv_hbm, wv), (wq_hbm, wq), (wo_hbm, wo)])
    ]
    for c in weight_copies:
        c.start()

    def cache_copies(d):
        return [
            pltpu.make_async_copy(
                cache_hbm.at[i, pl.ds(pl.multiple_of(WINDOW + (s - d) * TOK_DEV, TOK_DEV), TOK_DEV), :],
                kv.at[pl.ds(WINDOW - d * TOK_DEV, TOK_DEV), pl.ds(i * kv_width, kv_width)],
                cache_sem.at[d - 1, i],
            )
            for i in range(2)
        ]

    for d in range(1, REACH + 1):
        @pl.when(s < d)
        def _():
            for c in cache_copies(d):
                c.start()

    barrier = pltpu.get_barrier_semaphore()

    def greet(cond, ds, dz):
        @pl.when(cond)
        def _():
            pl.semaphore_signal(barrier, inc=1, device_id=(s + ds, z + dz), device_id_type=MESH)

    partners = [(z > 0, 0, -1), (z < n - 1, 0, 1)]
    for d in range(1, REACH + 1):
        partners += [(s >= d, -d, 0), (s + d < s_count, d, 0)]
    for p in partners:
        greet(*p)

    def norm_chunk(i, carry):
        r0 = pl.multiple_of(i * 16, 16)
        x = act_ref[pl.ds(r0, 16), :].astype(jnp.float32)
        y = x * lax.rsqrt(jnp.mean(x * x, axis=-1, keepdims=True) + EPSILON) * gain_ref[...].reshape(1, D)
        rows[z, pl.ds(r0, 16), :] = y.astype(jnp.bfloat16)
        return carry

    pl.semaphore_wait(barrier, sum(jnp.where(p[0], 1, 0) for p in partners))

    right = lax.rem(z + 1, n)
    left = lax.rem(z + n - 1, n)

    def ag_copy(direction, block, c):
        where = rows.at[block, pl.ds(c * CR, CR), :]
        return pltpu.make_async_remote_copy(
            src_ref=where, dst_ref=where,
            send_sem=ag_send.at[direction, block, c], recv_sem=ag_recv.at[direction, block, c],
            device_id=(s, right if direction == 0 else left), device_id_type=MESH,
        )

    def kv_copy(d, block):
        r0 = pl.multiple_of(block * R, R)
        return pltpu.make_async_remote_copy(
            src_ref=kv.at[pl.ds(WINDOW + r0, R), :],
            dst_ref=kv.at[pl.ds(WINDOW - d * TOK_DEV + r0, R), :],
            send_sem=kv_send.at[d - 1, block], recv_sem=kv_recv.at[d - 1, block],
            device_id=(lax.rem(s + d, s_count), z), device_id_type=MESH,
        )

    def rs_copy(direction, block, slot, c):
        where = slots.at[slot, c]
        return pltpu.make_async_remote_copy(
            src_ref=where, dst_ref=where,
            send_sem=rs_send.at[direction, block, c], recv_sem=rs_recv.at[direction, block, c],
            device_id=(s, right if direction == 0 else left), device_id_type=MESH,
        )

    def project(block):
        r0 = pl.multiple_of(block * R, R)
        cosine = cos_ref[pl.ds(r0, R), :]
        sine = sin_ref[pl.ds(r0, R), :]

        def run(w, tile, rotary, scale, dst, dst_r0, dst_c0):
            def one(i, carry):
                c0 = pl.multiple_of(i * tile, tile)
                t = jnp.dot(rows[block], w[:, pl.ds(c0, tile)], preferred_element_type=jnp.float32)
                for h in range(tile // HD):
                    u = t[:, h * HD:(h + 1) * HD]
                    if rotary:
                        u = u * cosine + pltpu.roll(u, HD // 2, 1) * sine
                    if scale is not None:
                        u = u * scale
                    dst[pl.ds(dst_r0, R), pl.ds(pl.multiple_of(dst_c0 + c0 + h * HD, HD), HD)] = u.astype(jnp.bfloat16)
                return carry
            lax.fori_loop(0, w.shape[1] // tile, one, 0)

        tile = min(256, kv_width)
        own = pl.multiple_of(WINDOW + r0, R)
        run(wk, tile, True, None, kv, own, 0)
        run(wv, tile, False, None, kv, own, kv_width)
        for d in range(1, REACH + 1):
            @pl.when(s + d < s_count)
            def _():
                kv_copy(d, block).start()
        run(wq, 256, True, SCALAR ** (-0.5), q_buf, r0, 0)

    for c in range(row_chunks):
        lax.fori_loop(c * CR // 16, (c + 1) * CR // 16, norm_chunk, 0)

        @pl.when(z < n - 1)
        def _():
            ag_copy(0, z, c).start()

        @pl.when(z > 0)
        def _():
            ag_copy(1, z, c).start()

    for i in range(3):
        weight_copies[i].wait()
    def gather_step(t, carry):
        from_left = z - t
        from_right = z + t
        for c in range(row_chunks):
            @pl.when(from_left >= 0)
            def _():
                ag_copy(0, from_left, c).wait_recv()

                @pl.when(z < n - 1)
                def _():
                    ag_copy(0, from_left, c).start()

            @pl.when(from_right < n)
            def _():
                ag_copy(1, from_right, c).wait_recv()

                @pl.when(z > 0)
                def _():
                    ag_copy(1, from_right, c).start()

            if c == 0:
                @pl.when(from_right - 1 < n)
                def _():
                    project(from_right - 1)

        @pl.when(from_left >= 0)
        def _():
            project(from_left)
        return carry

    lax.fori_loop(1, n, gather_step, 0)

    @pl.when(z == 0)
    def _():
        project(n - 1)

    for d in range(1, REACH + 1):
        @pl.when(s < d)
        def _():
            for c in cache_copies(d):
                c.wait()

        @pl.when(s >= d)
        def _():
            lax.fori_loop(0, n, lambda b, carry: (kv_copy(d, b).wait_recv(), carry)[1], 0)
    weight_copies[3].wait()

    row_i = lax.broadcasted_iota(jnp.int32, (group * R, R), 0)
    row_i = lax.rem(row_i, R)
    col_i = lax.broadcasted_iota(jnp.int32, (group * R, R), 1)
    later = col_i > row_i
    spans = [(0, R), (R, WINDOW - R), (WINDOW, R)]

    def attend(block):
        r0 = pl.multiple_of(block * R, R)
        for g in range(heads_kv):
            q = jnp.concatenate(
                [q_buf[pl.ds(r0, R), (g * group + a) * HD:(g * group + a + 1) * HD] for a in range(group)], axis=0
            )
            scores = []
            for j, (o, w) in enumerate(spans):
                k = kv[pl.ds(pl.multiple_of(r0 + o, R), w), g * HD:(g + 1) * HD]
                sc = lax.dot_general(q, k, (((1,), (1,)), ((), ())), preferred_element_type=jnp.float32)
                if j == 0:
                    sc = jnp.where(later, sc, -jnp.inf)
                if j == 2:
                    sc = jnp.where(later, -jnp.inf, sc)
                scores.append(sc)
            m = functools.reduce(jnp.maximum, [jnp.max(x, axis=-1, keepdims=True) for x in scores])
            total = 0.0
            o_sum = 0.0
            for (o, w), sc in zip(spans, scores):
                e = jnp.exp(sc - m)
                total = total + jnp.sum(e, axis=-1, keepdims=True)
                v = kv[pl.ds(pl.multiple_of(r0 + o, R), w), kv_width + g * HD:kv_width + (g + 1) * HD]
                o_sum = o_sum + jnp.dot(e.astype(jnp.bfloat16), v, preferred_element_type=jnp.float32)
            o_sum = (o_sum / total).astype(jnp.bfloat16)
            for a in range(group):
                att[:, (g * group + a) * HD:(g * group + a + 1) * HD] = o_sum[a * R:(a + 1) * R]

    TILE = 256

    def partial_out(direction, block, incoming):
        attend(block)
        for c in range(COL_CHUNKS):
            @pl.when(incoming)
            def _():
                rs_copy(direction, block, block, c).wait_recv()

            def one(i, carry):
                c0 = pl.multiple_of(i * TILE, TILE)
                w0 = pl.multiple_of(c * CD + i * TILE, TILE)
                p = jnp.dot(att[...], wo[:, pl.ds(w0, TILE)], preferred_element_type=jnp.float32)
                before = slots[block, c, :, pl.ds(c0, TILE)].astype(jnp.float32)
                p = p + jnp.where(incoming, before, 0.0)
                slots[block, c, :, pl.ds(c0, TILE)] = p.astype(jnp.bfloat16)
                return carry
            lax.fori_loop(0, CD // TILE, one, 0)
            send_out(direction, block, c).start()

    def send_out(direction, block, c):
        if direction == 0:
            return rs_copy(0, block, block, c)
        last = jnp.where(block == z - 1, n, block)
        return pltpu.make_async_remote_copy(
            src_ref=slots.at[block, c], dst_ref=slots.at[last, c],
            send_sem=rs_send.at[1, block, c], recv_sem=rs_recv.at[1, block, c],
            device_id=(s, left), device_id_type=MESH,
        )

    def scatter_step(t, carry):
        to_right = n - t
        to_left = t - 1

        @pl.when(to_right > z)
        def _():
            partial_out(0, to_right, z > 0)

        @pl.when(to_left < z)
        def _():
            partial_out(1, to_left, z < n - 1)
        return carry

    lax.fori_loop(1, n, scatter_step, 0)

    attend(z)

    def own(i, carry):
        w0 = pl.multiple_of(i * TILE, TILE)
        acc[:, pl.ds(w0, TILE)] = jnp.dot(att[...], wo[:, pl.ds(w0, TILE)], preferred_element_type=jnp.float32)
        return carry
    lax.fori_loop(0, D // TILE, own, 0)

    for c in range(COL_CHUNKS):
        for direction, slot, cond in ((0, z, z > 0), (1, n, z < n - 1)):
            @pl.when(cond)
            def _():
                rs_copy(direction, z, slot, c).wait_recv()
                acc[:, c * CD:(c + 1) * CD] += slots[slot, c].astype(jnp.float32)

    def finish(i, carry):
        r0 = pl.multiple_of(i * 16, 16)
        x = acc[pl.ds(r0, 16), :]
        y = x * lax.rsqrt(jnp.mean(x * x, axis=-1, keepdims=True) + EPSILON) * post_ref[...].reshape(1, D)
        out_ref[pl.ds(r0, 16), :] = (act_ref[pl.ds(r0, 16), :].astype(jnp.float32) + y).astype(jnp.bfloat16)
        return carry
    lax.fori_loop(0, R // 16, finish, 0)

    def drain(b, carry):
        @pl.when((b <= z) & (z < n - 1))
        def _():
            for c in range(row_chunks):
                ag_copy(0, b, c).wait_send()

        @pl.when((b >= z) & (z > 0))
        def _():
            for c in range(row_chunks):
                ag_copy(1, b, c).wait_send()

        @pl.when(b > z)
        def _():
            for c in range(COL_CHUNKS):
                send_out(0, b, c).wait_send()

        @pl.when(b < z)
        def _():
            for c in range(COL_CHUNKS):
                send_out(1, b, c).wait_send()

        for d in range(1, REACH + 1):
            @pl.when(s + d < s_count)
            def _():
                kv_copy(d, b).wait_send()
        return carry
    lax.fori_loop(0, n, drain, 0)


def per_device(n, s_count, act, gain, wq, wk, wv, wo, cache, post):
    R, D = act.shape
    row_chunks = min(4, R // 16)
    s = lax.axis_index("seq")
    positions = (s * TOK_DEV + jnp.arange(TOK_DEV, dtype=jnp.int32)).astype(jnp.float32)
    cosine, sine = rope_tables(positions)
    bf, f32 = jnp.bfloat16, jnp.float32
    vmem = pl.BlockSpec(memory_space=pltpu.VMEM)
    hbm = pl.BlockSpec(memory_space=pl.ANY)
    dma = pltpu.SemaphoreType.DMA
    return pl.pallas_call(
        functools.partial(kernel, n, s_count),
        out_shape=jax.ShapeDtypeStruct((R, D), bf),
        in_specs=[vmem, vmem, hbm, hbm, hbm, hbm, hbm, vmem, vmem, vmem],
        out_specs=vmem,
        scratch_shapes=[
            pltpu.VMEM(wq.shape, bf),
            pltpu.VMEM(wk.shape, bf),
            pltpu.VMEM(wv.shape, bf),
            pltpu.VMEM(wo.shape, bf),
            pltpu.VMEM((n, R, D), bf),
            pltpu.VMEM((TOK_DEV, wq.shape[1]), bf),
            pltpu.VMEM((WINDOW + TOK_DEV, 2 * wk.shape[1]), bf),
            pltpu.VMEM((R, wo.shape[0]), bf),
            pltpu.VMEM((n + 1, COL_CHUNKS, R, D // COL_CHUNKS), bf),
            pltpu.VMEM((R, D), f32),
            dma((4,)),
            dma((REACH, 2)),
            dma((2, n, row_chunks)),
            dma((2, n, row_chunks)),
            dma((REACH, n)),
            dma((REACH, n)),
            dma((2, n, COL_CHUNKS)),
            dma((2, n, COL_CHUNKS)),
        ],
        compiler_params=pltpu.CompilerParams(
            collective_id=0, has_side_effects=True, vmem_limit_bytes=62 * 1024 * 1024
        ),
    )(act, gain, wq, wk, wv, wo, cache, post, cosine, sine)


PHASES = 4
CHIPS = 4
CORES = 2


def phased_kernel(
    act_ref, gain_ref, wq_hbm, wk_hbm, wv_hbm, wo_hbm, cache_hbm, post_ref, far_cos, far_sin, low_cos, low_sin,
    out_ref,
    w, wo, act_in, rows, q_buf, kv, att, att_x, slots, acc, stage,
    w_sem, cache_sem, spread_send, spread_recv, ag_send, ag_recv, core_send, core_recv,
    kv_send, kv_recv, att_send, att_recv, rs_send, rs_recv, out_send, out_recv, go_sem,
):
    n = 4
    s = lax.axis_index("seq")
    z = lax.axis_index("head")
    c = s // CORES
    k = lax.rem(s, CORES)
    B, D = act_in.shape[1:]
    KW = wk_hbm.shape[1] // CORES
    QW = wq_hbm.shape[1] // CORES
    heads_kv = KW // HD
    group = QW // KW
    bf, f32 = jnp.bfloat16, jnp.float32
    near = z // 2
    inner = (z > 0) & (z < n - 1)
    outer = (z == 0) | (z == n - 1)

    def remote(src, dst, send, recv, chip, core, plane):
        return pltpu.make_async_remote_copy(
            src_ref=src, dst_ref=dst, send_sem=send, recv_sem=recv,
            device_id=(chip * CORES + core, plane), device_id_type=MESH,
        )

    def chip_at(d):
        return [c + 1 - 2 * lax.rem(c, 2), lax.rem(c + 2, CHIPS), CHIPS - 1 - c][d]

    weight_copies = [
        pltpu.make_async_copy(wk_hbm.at[:, pl.ds(pl.multiple_of(k * KW, KW), KW)], w.at[:, pl.ds(0, KW)], w_sem.at[0]),
        pltpu.make_async_copy(wv_hbm.at[:, pl.ds(pl.multiple_of(k * KW, KW), KW)], w.at[:, pl.ds(KW, KW)], w_sem.at[1]),
        pltpu.make_async_copy(wq_hbm.at[:, pl.ds(pl.multiple_of(k * QW, QW), QW)], w.at[:, pl.ds(2 * KW, QW)], w_sem.at[2]),
        pltpu.make_async_copy(wo_hbm, wo, w_sem.at[3]),
    ]
    cache_copies = [
        pltpu.make_async_copy(
            cache_hbm.at[i, :, :, :, :, pl.ds(pl.multiple_of(k * KW, KW), KW)],
            kv.at[pl.ds(0, 4), :, :, :, pl.ds(i * KW, KW)],
            cache_sem.at[i],
        )
        for i in range(2)
    ]

    barrier = pltpu.get_barrier_semaphore()

    def greet(chip, core, plane):
        pl.semaphore_signal(barrier, inc=1, device_id=(chip * CORES + core, plane), device_id_type=MESH)

    for d in range(3):
        greet(chip_at(d), k, z)
    greet(c, 1 - k, z)

    @pl.when(z > 0)
    def _():
        greet(c, k, z - 1)

    @pl.when(z < n - 1)
    def _():
        greet(c, k, z + 1)

    for x in weight_copies + cache_copies:
        x.start()
    pl.semaphore_wait(barrier, 4 + jnp.where(inner, 2, 1))

    H = B // 2

    def spread_copy(d, piece):
        to = chip_at(d)
        return remote(
            act_ref.at[pl.ds(pl.multiple_of(to * B + piece * H, H), H), :],
            act_in.at[c, pl.ds(piece * H, H), :],
            spread_send.at[d, piece], spread_recv.at[c, piece], to, k, z,
        )

    def spread_wait(t, piece):
        where = act_in.at[t, pl.ds(piece * H, H), :]
        remote(where, where, spread_send.at[0, piece], spread_recv.at[t, piece], c, k, z).wait_recv()

    def ag_copy(t, direction, zb, piece):
        where = rows.at[2 * t + k, zb, pl.ds(piece * H, H), :]
        to = jnp.minimum(z + 1, n - 1) if direction == 0 else jnp.maximum(z - 1, 0)
        return remote(where, where, ag_send.at[t, direction, zb, piece], ag_recv.at[t, zb, piece], c, k, to)

    def core_copy(u, zb, piece):
        where = rows.at[u, zb, pl.ds(piece * H, H), :]
        return remote(where, where, core_send.at[u // 2, zb, piece], core_recv.at[u // 2, zb, piece], c, 1 - k, z)

    def forward(t, zb, right, left, piece):
        if right:
            @pl.when(z < n - 1)
            def _():
                ag_copy(t, 0, zb, piece).start()
        if left:
            @pl.when(z > 0)
            def _():
                ag_copy(t, 1, zb, piece).start()
        core_copy(2 * t + k, zb, piece).start()

    def normalize_and_send(t):
        for piece in range(2):
            part = pl.ds(piece * H, H)

            @pl.when(t != c)
            def _():
                spread_wait(t, piece)

            x = act_in[t, part, :].astype(f32)
            y = x * lax.rsqrt(jnp.mean(x * x, axis=-1, keepdims=True) + EPSILON) * gain_ref[...].reshape(1, D)
            rows[2 * t + k, z, part, :] = y.astype(bf)
            forward(t, z, True, True, piece)

    def hop(t, h):
        @pl.when(z - h >= 0)
        def _():
            for piece in range(2):
                ag_copy(t, 0, z - h, piece).wait_recv()
                forward(t, z - h, True, False, piece)

        @pl.when(z + h < n)
        def _():
            for piece in range(2):
                ag_copy(t, 1, z + h, piece).wait_recv()
                forward(t, z + h, False, True, piece)

    def kv_copy(u, d, chip):
        where = kv.at[pl.ds(4 + 2 * u, 2), :, chip]
        return remote(where, where, kv_send.at[u, d], kv_recv.at[u, d], chip_at(d), k, z)

    def project(u):
        @pl.when(lax.rem(u, 2) != k)
        def _():
            for zb in range(n):
                for piece in range(2):
                    core_copy(u, zb, piece).wait_recv()

        cosine, sine = [], []
        for i in range(n):
            ca, sa = far_cos[4 * u + i], far_sin[4 * u + i]
            cb, sb = low_cos[...], low_sin[...]
            cosine.append(ca * cb - sa * sb)
            sine.append(sa * cb + ca * sb)
        cosine = jnp.concatenate(cosine, axis=0)
        sine = jnp.concatenate(sine, axis=0)

        def matmul(c0, width):
            return jnp.dot(
                rows[u].reshape(n * B, D), w[:, pl.ds(c0, width)], preferred_element_type=f32
            )

        def rope(x):
            return x * cosine + pltpu.roll(x, HD // 2, 1) * sine

        for part in range(2):
            x = matmul(part * KW, KW)
            for h in range(heads_kv):
                v = x[:, h * HD:(h + 1) * HD]
                v = (rope(v) if part == 0 else v).astype(bf)
                c0 = part * KW + h * HD
                for zb in range(n):
                    kv[4 + 2 * u + zb // 2, zb % 2, c, :, c0:c0 + HD] = v[zb * B:(zb + 1) * B]
        for d in range(3):
            kv_copy(u, 2 - d, c).start()

        def queries(i, carry):
            c0 = pl.multiple_of(i * 256, 256)
            x = matmul(2 * KW + c0, 256)
            for h in range(256 // HD):
                v = (rope(x[:, h * HD:(h + 1) * HD]) * SCALAR ** (-0.5)).astype(bf)
                for half in range(2):
                    q_buf[u, half, :, pl.ds(pl.multiple_of(c0 + h * HD, HD), HD)] = v[half * 2 * B:(half + 1) * 2 * B]
            return carry
        lax.fori_loop(0, QW // 256, queries, 0)

    M = group * 2 * B
    row = lax.rem(lax.broadcasted_iota(jnp.int32, (M, 256), 0), 2 * B)
    place = (row // B) * (CHIPS * B) + lax.rem(row, B) + c * B
    later = lax.broadcasted_iota(jnp.int32, (M, 256), 1) > place
    spans = [(0, 1), (1, 3), (4, 1)]

    def attend(unit, half, dst, dst_c0):
        t = unit // 2
        u = 2 * unit + half
        for g in range(heads_kv):
            q = jnp.concatenate(
                [q_buf[unit, half, :, (g * group + a) * HD:(g * group + a + 1) * HD] for a in range(group)], axis=0
            )
            scores = []
            for j, (o, wd) in enumerate(spans):
                key = kv[pl.ds(u + o, wd), :, :, :, g * HD:(g + 1) * HD].reshape(wd * 256, HD)
                sc = lax.dot_general(q, key, (((1,), (1,)), ((), ())), preferred_element_type=f32)
                if j == 0:
                    sc = jnp.where(later, sc, -jnp.inf)
                if j == 2:
                    sc = jnp.where(later, -jnp.inf, sc)
                scores.append(sc)
            m = functools.reduce(jnp.maximum, [jnp.max(x, axis=-1, keepdims=True) for x in scores])
            total = 0.0
            o_sum = 0.0
            for (o, wd), sc in zip(spans, scores):
                e = jnp.exp(sc - m)
                total = total + jnp.sum(e, axis=-1, keepdims=True)
                v = kv[pl.ds(u + o, wd), :, :, :, KW + g * HD:KW + (g + 1) * HD].reshape(wd * 256, HD)
                o_sum = o_sum + jnp.dot(e.astype(bf), v, preferred_element_type=f32)
            o_sum = (o_sum / total).astype(bf)
            for a in range(group):
                c0 = dst_c0 + (g * group + a) * HD
                dst[t, half, :, pl.ds(pl.multiple_of(c0, HD), HD)] = o_sum[a * 2 * B:(a + 1) * 2 * B]

    def attend_halves(u, dst, dst_c0):
        def one(half, carry):
            attend(u, half, dst, dst_c0)
            return carry
        lax.fori_loop(0, 2, one, 0)

    def att_copy(t, core):
        return remote(
            att_x.at[t], att.at[t, :, :, pl.ds(pl.multiple_of(core * QW, QW), QW)],
            att_send.at[t], att_recv.at[t], c, 1 - k, z,
        )

    TILE = 1792

    def project_out(t):
        def one(i, carry):
            w0 = pl.multiple_of(i * TILE, TILE)
            p = jnp.dot(att[t].reshape(n * B, CORES * QW), wo[:, pl.ds(w0, TILE)], preferred_element_type=f32)
            acc[lax.rem(t, 2), :, :, pl.ds(w0, TILE)] = p.reshape(n, B, TILE)
            return carry
        lax.fori_loop(0, D // TILE, one, 0)

    def relay_block(r):
        low = z < 2
        if r == 0:
            return jnp.where(low, n - 1, 0)
        if r == 1:
            return jnp.where(low, n - 2, 1)
        return z + 1 - 2 * lax.rem(z, 2)

    def rs_copy(t, b, piece):
        to = jnp.where(b > z, z + 1, z - 1)
        slot = jnp.where(b == z - 1, n, b)
        part = pl.ds(piece * H, H)
        return remote(
            slots.at[t, b, part, :], slots.at[t, slot, part, :],
            rs_send.at[t, b, piece], rs_recv.at[t, slot, piece], c, k, to,
        )

    def rs_wait(t, slot, piece):
        where = slots.at[t, slot, pl.ds(piece * H, H), :]
        remote(where, where, rs_send.at[t, 0, piece], rs_recv.at[t, slot, piece], c, k, z).wait_recv()

    WIDE = 1792

    def relay(t, r, incoming):
        b = relay_block(r)
        for piece in range(2):
            part = pl.ds(piece * H, H)
            if incoming:
                rs_wait(t, b, piece)

            def one(i, carry):
                c0 = pl.multiple_of(i * WIDE, WIDE)
                x = acc[lax.rem(t, 2), b, part, pl.ds(c0, WIDE)]
                if incoming:
                    x = x + slots[t, b, part, pl.ds(c0, WIDE)].astype(f32)
                slots[t, b, part, pl.ds(c0, WIDE)] = x.astype(bf)
                return carry
            lax.fori_loop(0, D // WIDE, one, 0)
            rs_copy(t, b, piece).start()

    def out_copy(t, piece):
        return remote(
            stage.at[t, pl.ds(piece * H, H), :],
            out_ref.at[pl.ds(pl.multiple_of(c * B + piece * H, H), H), :],
            out_send.at[t, piece], out_recv.at[c, piece], t, k, z,
        )

    def finish(t):
        for piece in range(2):
            @pl.when(z > 0)
            def _():
                rs_wait(t, z, piece)

            @pl.when(z < n - 1)
            def _():
                rs_wait(t, n, piece)

            part = pl.ds(piece * H, H)
            x = acc[lax.rem(t, 2), z, part, :]
            x = x + jnp.where(z > 0, slots[t, z, part, :].astype(f32), 0.0)
            x = x + jnp.where(z < n - 1, slots[t, n, part, :].astype(f32), 0.0)
            y = x * lax.rsqrt(jnp.mean(x * x, axis=-1, keepdims=True) + EPSILON) * post_ref[...].reshape(1, D)
            y = (act_in[t, part, :].astype(f32) + y).astype(bf)

            @pl.when(t == c)
            def _():
                out_ref[pl.ds(pl.multiple_of(c * B + piece * H, H), H), :] = y

            @pl.when(t != c)
            def _():
                stage[t, part, :] = y

            @pl.when(t != c)
            def _():
                out_copy(t, piece).start()

    def spread():
        for piece in range(2):
            for d in (2, 0, 1):
                spread_copy(d, piece).start()

    @pl.when((c == 0) & (k == 0))
    def _():
        spread()

    act_in[c] = act_ref[pl.ds(pl.multiple_of(c * B, B), B), :]
    normalize_and_send(c)

    @pl.when((c == 0) & (k == 0))
    def _():
        for d in range(3):
            for piece in range(2):
                spread_copy(d, piece).wait_send()
        pl.semaphore_signal(go_sem, inc=1, device_id=(s + 1, z), device_id_type=MESH)

    @pl.when((c == 0) & (k == 1))
    def _():
        pl.semaphore_wait(go_sem, 1)
        spread()

    @pl.when(c != 0)
    def _():
        @pl.when(k == 0)
        def _():
            normalize_and_send(0)
        spread()

    for x in cache_copies + weight_copies:
        x.wait()

    UNITS = PHASES * CORES

    def own_rows(t):
        @pl.when((t != c) & (t + k > 0))
        def _():
            normalize_and_send(t)

    def step(j, carry):
        mine = lax.rem(j, 2) == k
        gathers = mine & (j < UNITS)
        attends = (j >= 2) & (j <= UNITS + 1)
        sums = (~mine) & inner & (j >= 3)
        t = j // 2
        behind = (j - 3) // 2

        @pl.when(gathers)
        def _():
            hop(t, 1)

        @pl.when((~mine) & (j + 1 < UNITS) & (inner | (j == 0)))
        def _():
            own_rows((j + 1) // 2)

        @pl.when((j >= 1) & (j <= UNITS))
        def _():
            project(j - 1)

        @pl.when(attends)
        def _():
            for d in range(3):
                kv_copy(j - 2, d, chip_at(d)).wait_recv()

            @pl.when(~mine)
            def _():
                attend_halves(j - 2, att_x, 0)
                att_copy(t - 1, k).start()

            @pl.when(mine)
            def _():
                attend_halves(j - 2, att, k * QW)
                att_copy(t - 1, 1 - k).wait_recv()
                project_out(t - 1)

                @pl.when(outer)
                def _():
                    for r in range(3):
                        relay(t - 1, r, False)

        @pl.when(sums)
        def _():
            relay(behind, 0, True)

        @pl.when(gathers)
        def _():
            hop(t, 2)

        @pl.when(outer & mine & (j <= 1))
        def _():
            lax.fori_loop(1, PHASES, lambda q, carry: (own_rows(q), carry)[1], 0)

        @pl.when(sums)
        def _():
            relay(behind, 1, True)

        @pl.when(mine & (j >= 4))
        def _():
            finish(t - 2)

        @pl.when(gathers)
        def _():
            hop(t, 3)

        @pl.when(sums)
        def _():
            relay(behind, 2, True)
        return carry

    lax.fori_loop(0, UNITS + 3, step, 0)

    @pl.when(k == 1)
    def _():
        finish(PHASES - 1)

    for d in range(3):
        chip = chip_at(d)
        for piece in range(2):
            where = out_ref.at[pl.ds(pl.multiple_of(chip * B + piece * H, H), H), :]
            remote(where, where, out_send.at[0, piece], out_recv.at[chip, piece], c, k, z).wait_recv()

    @pl.when((c > 0) | (k > 0))
    def _():
        for d in range(3):
            for piece in range(2):
                spread_copy(d, piece).wait_send()

    def drain(t, carry):
        def blocks(b, carry):
            @pl.when((b <= z) & (z < n - 1))
            def _():
                for piece in range(2):
                    ag_copy(t, 0, b, piece).wait_send()

            @pl.when((b >= z) & (z > 0))
            def _():
                for piece in range(2):
                    ag_copy(t, 1, b, piece).wait_send()

            for piece in range(2):
                core_copy(2 * t + k, b, piece).wait_send()

            @pl.when(b != z)
            def _():
                for piece in range(2):
                    rs_copy(t, b, piece).wait_send()
            return carry
        lax.fori_loop(0, n, blocks, 0)
        for core in range(2):
            for d in range(3):
                kv_copy(2 * t + core, d, c).wait_send()
        att_copy(t, k).wait_send()

        @pl.when(t != c)
        def _():
            for piece in range(2):
                out_copy(t, piece).wait_send()
        return carry
    lax.fori_loop(0, PHASES, drain, 0)


def phased_per_device(act, gain, wq, wk, wv, wo, cache, post):
    R, D = act.shape
    n = 4
    B = R // CHIPS
    c = lax.axis_index("seq") // CORES
    starts = R * jnp.arange(PHASES * CORES * n, dtype=jnp.int32) + B * c
    positions = jnp.concatenate([starts.reshape(-1), jnp.arange(B, dtype=jnp.int32)])
    cosine, sine = rope_tables(positions.astype(jnp.float32))
    blocks = starts.size
    far = [x[:blocks].reshape(blocks, 1, HD) for x in (cosine, sine)]
    low = [x[blocks:] for x in (cosine, sine)]
    bf, f32 = jnp.bfloat16, jnp.float32
    vmem = pl.BlockSpec(memory_space=pltpu.VMEM)
    hbm = pl.BlockSpec(memory_space=pl.ANY)
    dma = pltpu.SemaphoreType.DMA
    KW, QW = wk.shape[1] // CORES, wq.shape[1] // CORES
    cache = cache.reshape(2, 4, 2, CHIPS, B, wk.shape[1])
    return pl.pallas_call(
        phased_kernel,
        out_shape=jax.ShapeDtypeStruct((R, D), bf),
        in_specs=[vmem, vmem, hbm, hbm, hbm, hbm, hbm, vmem, vmem, vmem, vmem, vmem],
        out_specs=vmem,
        scratch_shapes=[
            pltpu.VMEM((D, 2 * KW + QW), bf),
            pltpu.VMEM(wo.shape, bf),
            pltpu.VMEM((PHASES, B, D), bf),
            pltpu.VMEM((PHASES * CORES, n, B, D), bf),
            pltpu.VMEM((PHASES * CORES, 2, 2 * B, QW), bf),
            pltpu.VMEM((4 + 4 * PHASES, 2, CHIPS, B, 2 * KW), bf),
            pltpu.VMEM((PHASES, 2, 2 * B, CORES * QW), bf),
            pltpu.VMEM((PHASES, 2, 2 * B, QW), bf),
            pltpu.VMEM((PHASES, n + 1, B, D), bf),
            pltpu.VMEM((2, n, B, D), f32),
            pltpu.VMEM((PHASES, B, D), bf),
            dma((4,)),
            dma((2,)),
            dma((3, 2)),
            dma((CHIPS, 2)),
            dma((PHASES, 2, n, 2)),
            dma((PHASES, n, 2)),
            dma((PHASES, n, 2)),
            dma((PHASES, n, 2)),
            dma((PHASES * CORES, 3)),
            dma((PHASES * CORES, 3)),
            dma((PHASES,)),
            dma((PHASES,)),
            dma((PHASES, n, 2)),
            dma((PHASES, n + 1, 2)),
            dma((PHASES, 2)),
            dma((CHIPS, 2)),
            pltpu.SemaphoreType.REGULAR,
        ],
        compiler_params=pltpu.CompilerParams(
            collective_id=1, has_side_effects=True, vmem_limit_bytes=62 * 1024 * 1024
        ),
    )(act, gain, wq, wk, wv, wo, cache, post, *far, *low)


def solution(mesh):
    if mesh.shape["head"] == 4 and mesh.shape["seq"] == CHIPS * CORES:
        body = phased_per_device
    else:
        body = functools.partial(per_device, mesh.shape["head"], mesh.shape["seq"])
    return jax.shard_map(
        body,
        mesh=mesh,
        in_specs=(
            P(("seq", "head"), None),
            P(),
            P(None, "head"),
            P(None, "head"),
            P(None, "head"),
            P("head", None),
            P(None, None, "head"),
            P(),
        ),
        out_specs=P(("seq", "head"), None),
        check_vma=False,
    )
```
